512 devices in a mesh: row: 8 (over y), col: 16 (over z, core), layer: 4 (over x).
Axes of the slice: x: 4, y: 8, z: 8, core: 2. Of those that a mesh axis runs over, the one named last changes fastest.
Arguments:
- matrix: bfloat16 [6144, 6144], P('row', 'col'), may hold values from -2 to 2, as said below
- keep_mask: int32 [96, 96], P('row', 'col'), may hold values 0 or 1
- send_list: int32 [128, 16], P(('row', 'col')), may hold values from -1 to 71, as said below
Outputs:
- owned_blocks: bfloat16 [2048, 4096], P(('row', 'col'))
The draws below stay inside these ranges and needn't reach their ends.
Inputs may be any that keep to these rules, and one draw needn't show every extreme that they name: matrix is zero outside a block pattern except on its diagonal. send_list[s, e] numbers a block of source s's tile row-major over its 12 x (6) blocks, or is -1; a source names each block at most once; some owner column receives a block from every source of its grid row.
All inputs are finite; a program needn't handle non-finite values. No bound on the sum of `keep_mask` on one device may be relied on, other than what follows from the above.
Results may differ from the reference program's by a relative error of at most 0.0065.
Values may be sent and summed in bfloat16 or wider, within the bound.
No kernel may reach another device: no remote copies, remote signals or barrier semaphores. Data moves between devices by JAX's collectives and lax.ppermute only.
A program may use at most 64 MiB of HBM per device.

```python
import math
import jax
import jax.numpy as jnp

BLK = 64
TB = 12
NB = 96
ORDER = 6144
N_ROW = 8
N_COL = 16


def draw_matrix(key, part):
    key = jax.random.fold_in(key, 11)
    pattern_key, value_key, diag_key, sign_key = jax.random.split(key, 4)
    present = (jax.random.randint(pattern_key, (NB, NB), 0, 4) == 0).astype(jnp.float32)
    present = jnp.maximum(present, jnp.eye(NB, dtype=jnp.float32))
    spread = 1.0 / math.sqrt(16.0 * (NB + 3))
    values = jax.random.truncated_normal(value_key, -6.0, 6.0, (ORDER, ORDER), jnp.float32) * spread
    mask_full = jnp.repeat(jnp.repeat(present, BLK, 0), BLK, 1)
    magnitude = jax.random.uniform(diag_key, (ORDER,), jnp.float32, 0.5, 2.0) * spread
    signs = 2.0 * jax.random.randint(sign_key, (ORDER,), 0, 2).astype(jnp.float32) - 1.0
    return (values * mask_full + jnp.diag(magnitude * signs)).astype(jnp.bfloat16)


def draw_send_list(key, part):
    key = jax.random.fold_in(key, 23)
    devices = N_ROW * N_COL
    panel_blocks = TB * (TB // 2)
    most = min(panel_blocks, N_COL)
    count_key, full_key, owner_key, rows_key = jax.random.split(key, 4)
    counts = jax.random.randint(count_key, (devices,), most // 2, most + 1)
    full_source = jax.random.randint(full_key, (), 0, devices)
    counts = jnp.where(jnp.arange(devices) == full_source, most, counts)
    busiest = jax.random.randint(owner_key, (), 0, N_COL)
    padding = jnp.full((max(0, N_COL - panel_blocks),), -1, jnp.int32)

    def one_row(row_key, count):
        first_key, second_key = jax.random.split(row_key)
        others = (busiest + 1 + jax.random.permutation(first_key, N_COL - 1)) % N_COL
        owners = jnp.concatenate([busiest[None], others]).astype(jnp.int32)
        blocks = jax.random.permutation(second_key, panel_blocks).astype(jnp.int32)
        blocks = jnp.concatenate([blocks, padding])[:N_COL]
        position = jnp.arange(N_COL)
        values = jnp.where(position < count, blocks, -1).astype(jnp.int32)
        return jnp.full((N_COL,), -1, jnp.int32).at[owners].set(values)
    return jax.vmap(one_row)(jax.random.split(rows_key, devices), counts)


def with_ends(drawn, own_key, least, high):
    longest = drawn.shape.index(max(drawn.shape))
    spots = []
    for shift in (0, 1):
        where = [jax.random.randint(jax.random.fold_in(own_key, axis), (), 0, length) for axis, length in enumerate(drawn.shape)]
        where[longest] = (where[longest] + shift) % drawn.shape[longest]
        spots.append(tuple(where))
    return drawn.at[spots[0]].set(least).at[spots[1]].set(high)


def setup_inputs(seed: int = 0) -> dict:
    keys = jax.random.split(jax.random.key(seed), 4)
    return {
        "matrix": draw_matrix(jax.random.fold_in(keys[3], 71), 0),
        "keep_mask": with_ends((jax.random.randint(keys[1], (NB, NB), 0, 2) < 1).astype(jnp.int32), jax.random.fold_in(keys[1], 1), 0, 1),
        "send_list": draw_send_list(jax.random.fold_in(keys[3], 71), 0),
    }


def reference(matrix, keep_mask, send_list):
    square = jnp.dot(matrix, matrix, preferred_element_type=jnp.float32)
    block_keep = jnp.repeat(jnp.repeat(keep_mask.astype(jnp.float32), BLK, 0), BLK, 1)
    filtered = (square * block_keep).astype(jnp.bfloat16)
    cube = jnp.dot(matrix, filtered, preferred_element_type=jnp.float32)
    updated = (1.5 * matrix.astype(jnp.float32) - 0.5 * cube).astype(jnp.bfloat16)
    blocks_count = updated.shape[0] // BLK
    tiles = updated.reshape(blocks_count, BLK, blocks_count, BLK).transpose(0, 2, 1, 3)
    tiles = tiles.reshape(blocks_count * blocks_count, BLK * BLK)
    owner = jnp.arange(N_ROW * N_COL, dtype=jnp.int32)
    owner_row = owner // N_COL
    owner_col = owner % N_COL
    source_col = jnp.arange(N_COL, dtype=jnp.int32)
    source = (owner_row[:, None] * N_COL + source_col[None, :]).astype(jnp.int32)
    chosen = send_list[source, owner_col[:, None]]
    half_blocks = TB // 2
    safe_index = jnp.maximum(chosen, 0).astype(jnp.int32)
    global_row = owner_row[:, None] * TB + safe_index // half_blocks
    global_col = source_col[None, :] * half_blocks + safe_index % half_blocks
    flat_index = (global_row * blocks_count + global_col).astype(jnp.int32)
    picked = jnp.take(tiles, flat_index.reshape(-1), axis=0)
    live = chosen.reshape(-1) >= 0
    return jnp.where(live[:, None], picked, jnp.zeros_like(picked))
```

```python
import jax
import jax.numpy as jnp
from jax import lax
from jax.sharding import PartitionSpec as P

BLK = 64


def on_device(matrix, keep_mask, send_list):
    layers = lax.axis_size("layer")
    layer_index = lax.axis_index("layer")
    tile_rows, width = matrix.shape
    part = width // layers
    halves = tile_rows // width
    left_piece = lax.dynamic_slice_in_dim(matrix, layer_index * part, part, 1).T
    right_piece = lax.dynamic_slice_in_dim(
        matrix.reshape(halves, layers, part, width), layer_index, 1, 1
    ).reshape(halves * part, width)
    left_t = lax.all_gather(left_piece, "col", axis=0, tiled=True)
    right = lax.all_gather(right_piece, "row", axis=0, tiled=True)
    contract = (((0,), (0,)), ((), ()))
    square_part = lax.dot_general(left_t, right, contract, preferred_element_type=jnp.float32)
    square_part = square_part.reshape(halves, layers, part, width).transpose(1, 0, 2, 3)
    square_part = square_part.reshape(layers, halves * part, width).astype(jnp.bfloat16)
    parts = lax.all_to_all(square_part, "layer", split_axis=0, concat_axis=0, tiled=True)
    square = parts.astype(jnp.float32).sum(0)
    block_keep = jnp.repeat(jnp.repeat(keep_mask.astype(jnp.float32), BLK, 0), BLK, 1)
    block_keep = lax.dynamic_slice_in_dim(
        block_keep.reshape(halves, layers, part, width), layer_index, 1, 1
    ).reshape(halves * part, width)
    filtered_piece = (square * block_keep).astype(jnp.bfloat16)
    filtered = lax.all_gather(filtered_piece, "row", axis=0, tiled=True)
    cube_part = lax.dot_general(left_t, filtered, contract, preferred_element_type=jnp.float32)
    own = jnp.where(layer_index == 0, 1.5, 0.0) * matrix.astype(jnp.float32)
    updated = (own - 0.5 * cube_part).astype(jnp.bfloat16)
    tile_blocks = tile_rows // BLK
    half_blocks = width // BLK
    blocks = updated.reshape(tile_blocks, BLK, half_blocks, BLK).transpose(0, 2, 1, 3)
    blocks = blocks.reshape(tile_blocks * half_blocks, BLK * BLK // 128, 128)
    chosen = send_list[0]
    picked = jnp.take(blocks, jnp.maximum(chosen, 0), axis=0)
    outgoing = jnp.where((chosen >= 0)[:, None, None], picked, jnp.zeros_like(picked))
    arrived = lax.all_to_all(outgoing, "col", split_axis=0, concat_axis=0, tiled=True)
    everyone = lax.all_gather(arrived, "layer", axis=0)
    total = everyone.astype(jnp.float32).sum(0).astype(jnp.bfloat16)
    return total.reshape(total.shape[0], BLK * BLK)


def solution(mesh):
    in_specs = (P("row", "col"), P("row", "col"), P(("row", "col"), None))
    out_specs = P(("row", "col"), None)
    return jax.shard_map(
        on_device, mesh=mesh, in_specs=in_specs, out_specs=out_specs, check_vma=False
    )
```

```python
import functools

import jax
import jax.numpy as jnp
from jax import lax
from jax.experimental import pallas as pl
from jax.experimental.pallas import tpu as pltpu
from jax.sharding import Mesh, PartitionSpec as P

BLK = 64
CONTRACT = (((0,), (0,)), ((), ()))


def to_all(piece, axis):
    copies = jnp.broadcast_to(piece[None], (lax.axis_size(axis),) + piece.shape)
    return lax.all_to_all(copies, axis, split_axis=0, concat_axis=0, tiled=True)


def product(left_ref, right_ref):
    _, depth, _ = left_ref.shape
    columns = right_ref.shape[-1]
    total = None
    for side in range(2):
        right = right_ref[:, side].reshape(depth, columns)
        term = lax.dot_general(left_ref[side], right, CONTRACT, preferred_element_type=jnp.float32)
        total = term if total is None else total + term
    return total


def square_kernel(left_ref, right_ref, out_ref):
    layers, halves, part, columns = out_ref.shape
    total = product(left_ref, right_ref).astype(out_ref.dtype)
    for half in range(halves):
        for layer in range(layers):
            start = (half * layers + layer) * part
            out_ref[layer, half] = total[start : start + part]


def cube_kernel(chosen_ref, left_ref, right_ref, matrix_ref, own_ref, out_ref, total_ref, block_ref):
    owners, pairs, lanes = out_ref.shape
    half_blocks = matrix_ref.shape[1] // BLK
    total_ref[...] = own_ref[0] * matrix_ref[...].astype(jnp.float32) - 0.5 * product(left_ref, right_ref)
    low = lax.broadcasted_iota(jnp.int32, (pairs, lanes), 1) < BLK

    def one(owner, carry):
        index = chosen_ref[owner]
        live = jnp.where(index >= 0, 1.0, 0.0)
        index = jnp.maximum(index, 0)
        row = index // half_blocks
        column = index % half_blocks
        start = pl.multiple_of(row * BLK, BLK)
        lane = pl.multiple_of(column // 2 * lanes, lanes)
        block = total_ref[pl.ds(start, BLK), pl.ds(lane, lanes)] * live
        turned = pltpu.roll(block, BLK, 1)
        odd = column % 2 == 1
        block_ref[0] = jnp.where(odd, turned, block)
        block_ref[1] = jnp.where(odd, block, turned)
        even_rows = block_ref[0, pl.ds(0, pairs, stride=2), :]
        odd_rows = block_ref[1, pl.ds(1, pairs, stride=2), :]
        out_ref[owner] = jnp.where(low, even_rows, odd_rows).astype(out_ref.dtype)
        return carry

    lax.fori_loop(0, owners, one, 0)


def on_device(matrix, keep_mask, send_list):
    layers = lax.axis_size("layer")
    rows_count = lax.axis_size("row")
    layer_index = lax.axis_index("layer")
    core_index = lax.axis_index("core")
    tile_rows, width = matrix.shape
    part = width // layers
    halves = tile_rows // width
    depth = rows_count * part
    vmem = pl.BlockSpec(memory_space=pltpu.VMEM)
    smem = pl.BlockSpec(memory_space=pltpu.SMEM)
    params = pltpu.CompilerParams(vmem_limit_bytes=40 * 2**20)

    left_piece = lax.dynamic_slice_in_dim(matrix, layer_index * part, part, 1).T
    right_piece = lax.dynamic_slice_in_dim(
        matrix.reshape(halves, layers, part, width), layer_index, 1, 1
    ).reshape(halves, part, width)
    left_own = to_all(left_piece, "z").reshape(depth, tile_rows)
    right = to_all(right_piece, "row")
    left_other = lax.ppermute(left_own, "core", [(0, 1), (1, 0)])
    first = core_index == 0
    left = jnp.stack([jnp.where(first, left_own, left_other), jnp.where(first, left_other, left_own)])

    square_part = pl.pallas_call(
        square_kernel,
        out_shape=jax.ShapeDtypeStruct((layers, halves, part, width), jnp.bfloat16),
        in_specs=[vmem, vmem],
        out_specs=vmem,
        compiler_params=params,
    )(left, right)
    parts = lax.all_to_all(square_part, "layer", split_axis=0, concat_axis=0, tiled=True)
    square = parts.astype(jnp.float32).sum(0)
    block_keep = jnp.repeat(jnp.repeat(keep_mask.astype(jnp.float32), BLK, 0), BLK, 1)
    block_keep = lax.dynamic_slice_in_dim(
        block_keep.reshape(halves, layers, part, width), layer_index, 1, 1
    ).reshape(halves, part, width)
    filtered_piece = (square * block_keep).astype(jnp.bfloat16)
    filtered = to_all(filtered_piece, "row")

    own = jnp.where(layer_index == 0, 1.5, 0.0).astype(jnp.float32).reshape(1)
    chosen = send_list[0]
    pairs = BLK * BLK // 128
    outgoing = pl.pallas_call(
        cube_kernel,
        out_shape=jax.ShapeDtypeStruct((chosen.shape[0], pairs, 128), jnp.bfloat16),
        in_specs=[smem, vmem, vmem, vmem, smem],
        out_specs=vmem,
        scratch_shapes=[
            pltpu.VMEM((tile_rows, width), jnp.float32),
            pltpu.VMEM((2, BLK, 128), jnp.float32),
        ],
        compiler_params=params,
    )(chosen, left, filtered, matrix, own)
    arrived = lax.all_to_all(outgoing, ("z", "core"), split_axis=0, concat_axis=0, tiled=True)
    everyone = to_all(arrived, "layer")
    total = everyone.astype(jnp.float32).sum(0).astype(jnp.bfloat16)
    return total.reshape(total.shape[0], BLK * BLK)


def solution(mesh):
    sizes = mesh.shape
    cores = 2
    shape = (sizes["row"], sizes["col"] // cores, cores, sizes["layer"])
    split = Mesh(mesh.devices.reshape(shape), ("row", "z", "core", "layer"))
    column = ("z", "core")
    in_specs = (P("row", column), P("row", column), P(("row",) + column, None))
    out_specs = P(("row",) + column, None)
    return jax.shard_map(
        on_device, mesh=split, in_specs=in_specs, out_specs=out_specs, check_vma=False
    )
```

```python
import functools

import jax
import jax.numpy as jnp
from jax import lax
from jax.experimental import pallas as pl
from jax.experimental.pallas import tpu as pltpu
from jax.sharding import Mesh, PartitionSpec as P

BLK = 64
CONTRACT = (((0,), (0,)), ((), ()))


def to_all(piece, axis):
    copies = jnp.broadcast_to(piece[None], (lax.axis_size(axis),) + piece.shape)
    return lax.all_to_all(copies, axis, split_axis=0, concat_axis=0, tiled=True)


def shifted(piece, axis, by):
    size = lax.axis_size(axis)
    return lax.ppermute(piece, axis, [(i, (i - by) % size) for i in range(size)])


def ring_of_eight(piece, axis):
    half = piece.shape[0] // 2
    up = shifted(piece, axis, 2)
    down = shifted(piece, axis, -2)
    near_up = shifted(piece, axis, 1)
    near_down = shifted(piece, axis, -1)
    far_up = shifted(up, axis, 1)
    far_down = shifted(down, axis, -1)
    opposite_up = shifted(up[:half], axis, 2)
    opposite_down = shifted(down[half:], axis, -2)
    return piece, near_up, up, far_up, opposite_up, opposite_down, far_down, down, near_down


def product(own_ref, other_ref, right_ref):
    depth = own_ref.shape[0]
    columns = right_ref.shape[-1]
    own = lax.dot_general(
        own_ref[...], right_ref[0].reshape(depth, columns), CONTRACT, preferred_element_type=jnp.float32
    )
    other = lax.dot_general(
        other_ref[...], right_ref[1].reshape(depth, columns), CONTRACT, preferred_element_type=jnp.float32
    )
    return own + other


def square_kernel(place_ref, own_ref, other_ref, right_ref, out_ref, ordered_ref):
    layers, halves, part, columns = out_ref.shape
    tiles = right_ref.shape[0]
    z, core = place_ref[1], place_ref[2]
    for offset in range(tiles):
        tile = lax.rem(z + offset, tiles)
        ordered_ref[0, offset] = right_ref[tile, core]
        ordered_ref[1, offset] = right_ref[tile, 1 - core]
    total = product(own_ref, other_ref, ordered_ref).astype(out_ref.dtype)
    for half in range(halves):
        for layer in range(layers):
            start = (half * layers + layer) * part
            out_ref[layer, half] = total[start : start + part]


def cube_kernel(chosen_ref, place_ref, scale_ref, own_ref, other_ref, matrix_ref, *refs):
    pieces = refs[:9]
    out_ref, ordered_ref, total_ref, block_ref = refs[9:]
    tiles = ordered_ref.shape[1]
    row, z, core = place_ref[0], place_ref[1], place_ref[2]
    for offset, piece in zip((0, 1, 2, 3, 5, 6, 7), pieces[:4] + pieces[6:]):
        tile = lax.rem(row + offset + tiles - z, tiles)
        ordered_ref[0, tile] = piece[core]
        ordered_ref[1, tile] = piece[1 - core]
    tile = lax.rem(row + 4 + tiles - z, tiles)
    ordered_ref[core, tile] = pieces[4][0]
    ordered_ref[1 - core, tile] = pieces[5][0]
    owners, pairs, lanes = out_ref.shape
    half_blocks = matrix_ref.shape[1] // BLK
    total_ref[...] = scale_ref[0] * matrix_ref[...].astype(jnp.float32) - 0.5 * product(
        own_ref, other_ref, ordered_ref
    )
    low = lax.broadcasted_iota(jnp.int32, (pairs, lanes), 1) < BLK

    def one(owner, carry):
        index = chosen_ref[owner]
        live = jnp.where(index >= 0, 1.0, 0.0)
        index = jnp.maximum(index, 0)
        column = index % half_blocks
        start = pl.multiple_of(index // half_blocks * BLK, BLK)
        lane = pl.multiple_of(column // 2 * lanes, lanes)
        block = total_ref[pl.ds(start, BLK), pl.ds(lane, lanes)] * live
        turned = pltpu.roll(block, BLK, 1)
        odd = column % 2 == 1
        block_ref[0] = jnp.where(odd, turned, block)
        block_ref[1] = jnp.where(odd, block, turned)
        even_rows = block_ref[0, pl.ds(0, pairs, stride=2), :]
        odd_rows = block_ref[1, pl.ds(1, pairs, stride=2), :]
        out_ref[owner] = jnp.where(low, even_rows, odd_rows).astype(out_ref.dtype)
        return carry

    lax.fori_loop(0, owners, one, 0)


def on_device(matrix, keep_mask, send_list):
    layers = lax.axis_size("layer")
    rows_count = lax.axis_size("row")
    layer_index = lax.axis_index("layer")
    row_index = lax.axis_index("row")
    z_index = lax.axis_index("z")
    core_index = lax.axis_index("core")
    tile_rows, width = matrix.shape
    part = width // layers
    halves = tile_rows // width
    vmem = pl.BlockSpec(memory_space=pltpu.VMEM)
    smem = pl.BlockSpec(memory_space=pltpu.SMEM)
    params = pltpu.CompilerParams(vmem_limit_bytes=40 * 2**20)

    left_piece = lax.dynamic_slice_in_dim(matrix, layer_index * part, part, 1).T
    right_piece = lax.dynamic_slice_in_dim(
        matrix.reshape(halves, layers, part, width), layer_index, 1, 1
    ).reshape(halves, part, width)
    right = to_all(right_piece, "row")
    left_own = jnp.concatenate(ring_of_eight(left_piece, "z"), axis=0)
    left_other = lax.ppermute(left_own, "core", [(0, 1), (1, 0)])
    place = jnp.stack([row_index, z_index, core_index])

    square_part = pl.pallas_call(
        square_kernel,
        out_shape=jax.ShapeDtypeStruct((layers, halves, part, width), jnp.bfloat16),
        in_specs=[smem, vmem, vmem, vmem],
        out_specs=vmem,
        scratch_shapes=[pltpu.VMEM((halves, rows_count, part, width), jnp.bfloat16)],
        compiler_params=params,
    )(place, left_own, left_other, right)
    parts = lax.all_to_all(square_part, "layer", split_axis=0, concat_axis=0, tiled=True)
    square = parts.astype(jnp.float32).sum(0)
    block_keep = jnp.repeat(jnp.repeat(keep_mask.astype(jnp.float32), BLK, 0), BLK, 1)
    block_keep = lax.dynamic_slice_in_dim(
        block_keep.reshape(halves, layers, part, width), layer_index, 1, 1
    ).reshape(halves, part, width)
    filtered_piece = (square * block_keep).astype(jnp.bfloat16)
    filtered = ring_of_eight(filtered_piece, "row")

    scale = jnp.where(layer_index == 0, 1.5, 0.0).astype(jnp.float32).reshape(1)
    chosen = send_list[0]
    pairs = BLK * BLK // 128
    outgoing = pl.pallas_call(
        cube_kernel,
        out_shape=jax.ShapeDtypeStruct((chosen.shape[0], pairs, 128), jnp.bfloat16),
        in_specs=[smem] * 3 + [vmem] * 12,
        out_specs=vmem,
        scratch_shapes=[
            pltpu.VMEM((halves, rows_count, part, width), jnp.bfloat16),
            pltpu.VMEM((tile_rows, width), jnp.float32),
            pltpu.VMEM((2, BLK, 128), jnp.float32),
        ],
        compiler_params=params,
    )(chosen, place, scale, left_own, left_other, matrix, *filtered)
    arrived = lax.all_to_all(outgoing, ("z", "core"), split_axis=0, concat_axis=0, tiled=True)
    everyone = to_all(arrived, "layer")
    total = everyone.astype(jnp.float32).sum(0).astype(jnp.bfloat16)
    return total.reshape(total.shape[0], BLK * BLK)


def solution(mesh):
    sizes = mesh.shape
    cores = 2
    shape = (sizes["row"], sizes["col"] // cores, cores, sizes["layer"])
    split = Mesh(mesh.devices.reshape(shape), ("row", "z", "core", "layer"))
    column = ("z", "core")
    in_specs = (P("row", column), P("row", column), P(("row",) + column, None))
    out_specs = P(("row",) + column, None)
    return jax.shard_map(
        on_device, mesh=split, in_specs=in_specs, out_specs=out_specs, check_vma=False
    )
```

```python
import jax
import jax.numpy as jnp
from jax import lax
from jax.experimental import pallas as pl
from jax.experimental.pallas import tpu as pltpu
from jax.sharding import Mesh, PartitionSpec as P

BLK = 64
CONTRACT = (((0,), (0,)), ((), ()))


def to_all(piece, axis):
    copies = jnp.broadcast_to(piece[None], (lax.axis_size(axis),) + piece.shape)
    return lax.all_to_all(copies, axis, split_axis=0, concat_axis=0, tiled=True)


def shifted(piece, axis, by):
    size = lax.axis_size(axis)
    pairs = []
    for i in range(size):
        pairs.append((2 * i, 2 * ((i - by) % size)))
        pairs.append((2 * i + 1, 2 * ((i + by) % size) + 1))
    return lax.ppermute(piece, (axis, "core"), pairs)


def ring_of_eight(piece, axis):
    up = shifted(piece, axis, 2)
    down = shifted(piece, axis, -2)
    near_up = shifted(piece, axis, 1)
    near_down = shifted(piece, axis, -1)
    far_up = shifted(up, axis, 1)
    far_down = shifted(down, axis, -1)
    opposite = shifted(up, axis, 2)
    return piece, near_up, up, far_up, opposite, far_down, down, near_down


def product(own_ref, other_ref, right_ref, start, count):
    depth = own_ref.shape[0]
    columns = right_ref.shape[-1]
    rows = pl.ds(start, count)
    own = lax.dot_general(
        own_ref[:, rows], right_ref[0].reshape(depth, columns), CONTRACT, preferred_element_type=jnp.float32
    )
    other = lax.dot_general(
        other_ref[:, rows], right_ref[1].reshape(depth, columns), CONTRACT, preferred_element_type=jnp.float32
    )
    return own + other


def square_kernel(place_ref, own_ref, other_ref, right_ref, out_ref, ordered_ref, staged_ref, sems):
    halves, layers, part, columns = staged_ref.shape
    tiles = right_ref.shape[0]
    z, core = place_ref[1], place_ref[2]
    way = 1 - 2 * core
    for offset in range(tiles):
        ordered_ref[0, offset] = right_ref[lax.rem(z + way * offset + tiles, tiles), core]
        ordered_ref[1, offset] = right_ref[lax.rem(z - way * offset + tiles, tiles), 1 - core]
    copies = []
    for half in range(halves):
        count = layers * part
        total = product(own_ref, other_ref, ordered_ref, half * count, count)
        staged_ref[half] = total.astype(staged_ref.dtype).reshape(layers, part, columns)
        copies.append(pltpu.make_async_copy(staged_ref.at[half], out_ref.at[:, half], sems.at[half]))
        copies[-1].start()
    for copy in copies:
        copy.wait()


def filter_kernel(keep_ref, layer_ref, parts_ref, out_ref):
    layers, halves, part, columns = parts_ref.shape
    chunk = BLK // 2
    low = lax.broadcasted_iota(jnp.int32, (chunk, 2 * BLK), 1) < BLK
    for half in range(halves):
        for start in range(0, part, chunk):
            block = (half * layers * part + layer_ref[0] * part + start) // BLK
            rows = pl.ds(start, chunk)
            for lane in range(0, columns, 2 * BLK):
                lanes = pl.ds(lane, 2 * BLK)
                total = parts_ref[0, half, rows, lanes].astype(jnp.float32)
                for layer in range(1, layers):
                    total = total + parts_ref[layer, half, rows, lanes].astype(jnp.float32)
                left = keep_ref[block, lane // BLK].astype(jnp.float32)
                right = keep_ref[block, lane // BLK + 1].astype(jnp.float32)
                out_ref[half, rows, lanes] = (total * jnp.where(low, left, right)).astype(out_ref.dtype)


def cube_kernel(chosen_ref, place_ref, scale_ref, own_ref, other_ref, matrix_ref, *refs):
    pieces = refs[:8]
    out_ref, ordered_ref, total_ref, block_ref = refs[8:]
    owners, pairs, lanes = out_ref.shape
    half_blocks = matrix_ref.shape[1] // BLK
    tiles = ordered_ref.shape[1]
    row, z, core = place_ref[0], place_ref[1], place_ref[2]
    way = 1 - 2 * core
    for offset, piece in enumerate(pieces):
        distance = row + way * offset - z
        own = lax.rem(way * distance + 2 * tiles, tiles)
        ordered_ref[0, own] = piece[core]
        ordered_ref[1, lax.rem(tiles - own, tiles)] = piece[1 - core]
    total_ref[...] = scale_ref[0] * matrix_ref[...].astype(jnp.float32) - 0.5 * product(
        own_ref, other_ref, ordered_ref, 0, matrix_ref.shape[0]
    )
    low = lax.broadcasted_iota(jnp.int32, (pairs, lanes), 1) < BLK

    for owner in range(owners):
        index = chosen_ref[owner]
        live = jnp.where(index >= 0, 1.0, 0.0)
        index = jnp.maximum(index, 0)
        column = index % half_blocks
        start = pl.multiple_of(index // half_blocks * BLK, BLK)
        lane = pl.multiple_of(column // 2 * lanes, lanes)
        block = total_ref[pl.ds(start, BLK), pl.ds(lane, lanes)] * live
        turned = pltpu.roll(block, BLK, 1)
        odd = column % 2 == 1
        slot = 2 * (owner % 2)
        block_ref[slot] = jnp.where(odd, turned, block)
        block_ref[slot + 1] = jnp.where(odd, block, turned)
        even_rows = block_ref[slot, pl.ds(0, pairs, stride=2), :]
        odd_rows = block_ref[slot + 1, pl.ds(1, pairs, stride=2), :]
        out_ref[owner] = jnp.where(low, even_rows, odd_rows).astype(out_ref.dtype)


def on_device(matrix, keep_mask, send_list):
    layers = lax.axis_size("layer")
    rows_count = lax.axis_size("row")
    layer_index = lax.axis_index("layer")
    row_index = lax.axis_index("row")
    z_index = lax.axis_index("z")
    core_index = lax.axis_index("core")
    tile_rows, width = matrix.shape
    part = width // layers
    halves = tile_rows // width
    vmem = pl.BlockSpec(memory_space=pltpu.VMEM)
    smem = pl.BlockSpec(memory_space=pltpu.SMEM)
    params = pltpu.CompilerParams(vmem_limit_bytes=40 * 2**20)

    left_piece = lax.dynamic_slice_in_dim(matrix, layer_index * part, part, 1).T
    right_piece = lax.dynamic_slice_in_dim(
        matrix.reshape(halves, layers, part, width), layer_index, 1, 1
    ).reshape(halves, part, width)
    right = to_all(right_piece, "row")
    left_own = jnp.concatenate(ring_of_eight(left_piece, "z"), axis=0)
    left_own, right = lax.optimization_barrier((left_own, right))
    left_other = lax.ppermute(left_own, "core", [(0, 1), (1, 0)])
    place = jnp.stack([row_index, z_index, core_index])

    square_part = pl.pallas_call(
        square_kernel,
        out_shape=jax.ShapeDtypeStruct((layers, halves, part, width), jnp.bfloat16),
        in_specs=[smem, vmem, vmem, vmem],
        out_specs=pl.BlockSpec(memory_space=pltpu.HBM),
        scratch_shapes=[
            pltpu.VMEM((halves, rows_count, part, width), jnp.bfloat16),
            pltpu.VMEM((halves, layers, part, width), jnp.bfloat16),
            pltpu.SemaphoreType.DMA((halves,)),
        ],
        compiler_params=params,
    )(place, left_own, left_other, right)
    parts = lax.all_to_all(square_part, "layer", split_axis=0, concat_axis=0, tiled=True)
    filtered_piece = pl.pallas_call(
        filter_kernel,
        out_shape=jax.ShapeDtypeStruct((halves, part, width), jnp.bfloat16),
        in_specs=[smem, smem, vmem],
        out_specs=vmem,
        compiler_params=params,
    )(keep_mask, layer_index.reshape(1), parts)
    filtered = ring_of_eight(filtered_piece, "row")

    scale = jnp.where(layer_index == 0, 1.5, 0.0).astype(jnp.float32).reshape(1)
    chosen = send_list[0]
    pairs = BLK * BLK // 128
    outgoing = pl.pallas_call(
        cube_kernel,
        out_shape=jax.ShapeDtypeStruct((chosen.shape[0], pairs, 128), jnp.bfloat16),
        in_specs=[smem] * 3 + [vmem] * 11,
        out_specs=vmem,
        scratch_shapes=[
            pltpu.VMEM((halves, rows_count, part, width), jnp.bfloat16),
            pltpu.VMEM((tile_rows, width), jnp.float32),
            pltpu.VMEM((4, BLK, 128), jnp.float32),
        ],
        compiler_params=params,
    )(chosen, place, scale, left_own, left_other, matrix, *filtered)
    arrived = lax.all_to_all(outgoing, ("z", "core"), split_axis=0, concat_axis=0, tiled=True)
    everyone = to_all(arrived, "layer")
    total = everyone.astype(jnp.float32).sum(0).astype(jnp.bfloat16)
    return total.reshape(total.shape[0], BLK * BLK)


def solution(mesh):
    sizes = mesh.shape
    cores = 2
    shape = (sizes["row"], sizes["col"] // cores, cores, sizes["layer"])
    split = Mesh(mesh.devices.reshape(shape), ("row", "z", "core", "layer"))
    column = ("z", "core")
    in_specs = (P("row", column), P("row", column), P(("row",) + column, None))
    out_specs = P(("row",) + column, None)
    return jax.shard_map(
        on_device, mesh=split, in_specs=in_specs, out_specs=out_specs, check_vma=False
    )
```

```python
import jax
import jax.numpy as jnp
from jax import lax
from jax.experimental import pallas as pl
from jax.experimental.pallas import tpu as pltpu
from jax.sharding import Mesh, PartitionSpec as P

BLK = 64
CONTRACT = (((0,), (0,)), ((), ()))


def shifted(piece, axis, by):
    size = lax.axis_size(axis)
    pairs = []
    for i in range(size):
        pairs.append((2 * i, 2 * ((i - by) % size)))
        pairs.append((2 * i + 1, 2 * ((i + by) % size) + 1))
    return lax.ppermute(piece, (axis, "core"), pairs)


def rings_of_eight(pieces, axes):
    def step(held, by):
        got = [shifted(piece, axis, by) for piece, axis in zip(held, axes)]
        return lax.optimization_barrier(got) if len(got) > 1 else got

    ups = step(pieces, 2)
    downs = step(pieces, -2)
    near_ups = step(pieces, 1)
    near_downs = step(pieces, -1)
    far_ups = step(ups, 1)
    opposites = step(ups, 2)
    far_downs = step(downs, -1)
    return list(zip(pieces, near_ups, ups, far_ups, opposites, far_downs, downs, near_downs))


def put_in_order(place_ref, pieces, ordered_ref):
    tiles = ordered_ref.shape[1]
    row, z, core = place_ref[0], place_ref[1], place_ref[2]
    way = 1 - 2 * core
    for offset, piece in enumerate(pieces):
        distance = row + way * offset - z
        own = lax.rem(way * distance + 2 * tiles, tiles)
        ordered_ref[0, own] = piece[core]
        ordered_ref[1, lax.rem(tiles - own, tiles)] = piece[1 - core]


def product(own_ref, other_ref, right_ref, start, count):
    depth = own_ref.shape[0]
    columns = right_ref.shape[-1]
    rows = pl.ds(start, count)
    own = lax.dot_general(
        own_ref[:, rows], right_ref[0].reshape(depth, columns), CONTRACT, preferred_element_type=jnp.float32
    )
    other = lax.dot_general(
        other_ref[:, rows], right_ref[1].reshape(depth, columns), CONTRACT, preferred_element_type=jnp.float32
    )
    return own + other


def square_kernel(place_ref, own_ref, other_ref, *refs):
    out_ref, ordered_ref, staged_ref, sems = refs[8:]
    halves, layers, part, columns = staged_ref.shape
    put_in_order(place_ref, refs[:8], ordered_ref)
    copies = []
    for half in range(halves):
        count = layers * part
        total = product(own_ref, other_ref, ordered_ref, half * count, count)
        staged_ref[half] = total.astype(staged_ref.dtype).reshape(layers, part, columns)
        copies.append(pltpu.make_async_copy(staged_ref.at[half], out_ref.at[:, half], sems.at[half]))
        copies[-1].start()
    for copy in copies:
        copy.wait()


def filter_kernel(keep_ref, layer_ref, parts_ref, out_ref):
    layers, halves, part, columns = parts_ref.shape
    chunk = BLK // 2
    low = lax.broadcasted_iota(jnp.int32, (chunk, 2 * BLK), 1) < BLK
    for half in range(halves):
        for start in range(0, part, chunk):
            block = (half * layers * part + layer_ref[0] * part + start) // BLK
            rows = pl.ds(start, chunk)
            for lane in range(0, columns, 2 * BLK):
                lanes = pl.ds(lane, 2 * BLK)
                total = parts_ref[0, half, rows, lanes].astype(jnp.float32)
                for layer in range(1, layers):
                    total = total + parts_ref[layer, half, rows, lanes].astype(jnp.float32)
                left = keep_ref[block, lane // BLK].astype(jnp.float32)
                right = keep_ref[block, lane // BLK + 1].astype(jnp.float32)
                out_ref[half, rows, lanes] = (total * jnp.where(low, left, right)).astype(out_ref.dtype)


def cube_kernel(chosen_ref, place_ref, scale_ref, own_ref, other_ref, matrix_ref, *refs):
    pieces = refs[:8]
    out_ref, ordered_ref, total_ref, block_ref = refs[8:]
    owners, pairs, lanes = out_ref.shape
    half_blocks = matrix_ref.shape[1] // BLK
    put_in_order(place_ref, pieces, ordered_ref)
    total_ref[...] = scale_ref[0] * matrix_ref[...].astype(jnp.float32) - 0.5 * product(
        own_ref, other_ref, ordered_ref, 0, matrix_ref.shape[0]
    )
    low = lax.broadcasted_iota(jnp.int32, (pairs, lanes), 1) < BLK

    for owner in range(owners):
        index = chosen_ref[owner]
        live = jnp.where(index >= 0, 1.0, 0.0)
        index = jnp.maximum(index, 0)
        column = index % half_blocks
        start = pl.multiple_of(index // half_blocks * BLK, BLK)
        lane = pl.multiple_of(column // 2 * lanes, lanes)
        block = total_ref[pl.ds(start, BLK), pl.ds(lane, lanes)] * live
        turned = pltpu.roll(block, BLK, 1)
        odd = column % 2 == 1
        slot = 2 * (owner % 2)
        block_ref[slot] = jnp.where(odd, turned, block)
        block_ref[slot + 1] = jnp.where(odd, block, turned)
        even_rows = block_ref[slot, pl.ds(0, pairs, stride=2), :]
        odd_rows = block_ref[slot + 1, pl.ds(1, pairs, stride=2), :]
        out_ref[owner] = jnp.where(low, even_rows, odd_rows).astype(out_ref.dtype)


def on_device(matrix, keep_mask, send_list):
    layers = lax.axis_size("layer")
    rows_count = lax.axis_size("row")
    layer_index = lax.axis_index("layer")
    row_index = lax.axis_index("row")
    z_index = lax.axis_index("z")
    core_index = lax.axis_index("core")
    tile_rows, width = matrix.shape
    part = width // layers
    halves = tile_rows // width
    vmem = pl.BlockSpec(memory_space=pltpu.VMEM)
    smem = pl.BlockSpec(memory_space=pltpu.SMEM)
    params = pltpu.CompilerParams(vmem_limit_bytes=40 * 2**20)

    left_piece = lax.dynamic_slice_in_dim(matrix, layer_index * part, part, 1).T
    right_piece = lax.dynamic_slice_in_dim(
        matrix.reshape(halves, layers, part, width), layer_index, 1, 1
    ).reshape(halves, part, width)
    left_pieces, right = rings_of_eight((left_piece, right_piece), ("z", "row"))
    left_own = jnp.concatenate(left_pieces, axis=0)
    left_own, right = lax.optimization_barrier((left_own, right))
    left_other = lax.ppermute(left_own, "core", [(0, 1), (1, 0)])
    place = jnp.stack([row_index, z_index, core_index])

    square_part = pl.pallas_call(
        square_kernel,
        out_shape=jax.ShapeDtypeStruct((layers, halves, part, width), jnp.bfloat16),
        in_specs=[smem] + [vmem] * 10,
        out_specs=pl.BlockSpec(memory_space=pltpu.HBM),
        scratch_shapes=[
            pltpu.VMEM((halves, rows_count, part, width), jnp.bfloat16),
            pltpu.VMEM((halves, layers, part, width), jnp.bfloat16),
            pltpu.SemaphoreType.DMA((halves,)),
        ],
        compiler_params=params,
    )(place, left_own, left_other, *right)
    parts = lax.all_to_all(square_part, "layer", split_axis=0, concat_axis=0, tiled=True)
    filtered_piece = pl.pallas_call(
        filter_kernel,
        out_shape=jax.ShapeDtypeStruct((halves, part, width), jnp.bfloat16),
        in_specs=[smem, smem, vmem],
        out_specs=vmem,
        compiler_params=params,
    )(keep_mask, layer_index.reshape(1), parts)
    filtered = rings_of_eight((filtered_piece,), ("row",))[0]

    scale = jnp.where(layer_index == 0, 1.5, 0.0).astype(jnp.float32).reshape(1)
    chosen = send_list[0]
    pairs = BLK * BLK // 128
    outgoing = pl.pallas_call(
        cube_kernel,
        out_shape=jax.ShapeDtypeStruct((chosen.shape[0], pairs, 128), jnp.bfloat16),
        in_specs=[smem] * 3 + [vmem] * 11,
        out_specs=vmem,
        scratch_shapes=[
            pltpu.VMEM((halves, rows_count, part, width), jnp.bfloat16),
            pltpu.VMEM((tile_rows, width), jnp.float32),
            pltpu.VMEM((4, BLK, 128), jnp.float32),
        ],
        compiler_params=params,
    )(chosen, place, scale, left_own, left_other, matrix, *filtered)
    copies = jnp.broadcast_to(outgoing[:, None], outgoing.shape[:1] + (layers,) + outgoing.shape[1:])
    copies = copies.reshape((-1,) + outgoing.shape[1:])
    everyone = lax.all_to_all(copies, ("z", "core", "layer"), split_axis=0, concat_axis=0, tiled=True)
    everyone = everyone.reshape(outgoing.shape[:1] + (layers,) + outgoing.shape[1:])
    total = everyone.astype(jnp.float32).sum(1).astype(jnp.bfloat16)
    return total.reshape(total.shape[0], BLK * BLK)


def solution(mesh):
    sizes = mesh.shape
    cores = 2
    shape = (sizes["row"], sizes["col"] // cores, cores, sizes["layer"])
    split = Mesh(mesh.devices.reshape(shape), ("row", "z", "core", "layer"))
    column = ("z", "core")
    in_specs = (P("row", column), P("row", column), P(("row",) + column, None))
    out_specs = P(("row",) + column, None)
    return jax.shard_map(
        on_device, mesh=split, in_specs=in_specs, out_specs=out_specs, check_vma=False
    )
```

```python
import jax
import jax.numpy as jnp
from jax import lax
from jax.experimental import pallas as pl
from jax.experimental.pallas import tpu as pltpu
from jax.sharding import Mesh, PartitionSpec as P

BLK = 64
LAST = 5
CONTRACT = (((0,), (0,)), ((), ()))


def to_all(piece, axis):
    copies = jnp.broadcast_to(piece[None], (lax.axis_size(axis),) + piece.shape)
    return lax.all_to_all(copies, axis, split_axis=0, concat_axis=0, tiled=True)


def shifted(piece, axis, by):
    size = lax.axis_size(axis)
    pairs = []
    for i in range(size):
        pairs.append((2 * i, 2 * ((i - by) % size)))
        pairs.append((2 * i + 1, 2 * ((i + by) % size) + 1))
    return lax.ppermute(piece, (axis, "core"), pairs)


def ring_of_eight(piece, axis):
    up = shifted(piece, axis, 2)
    down = shifted(piece, axis, -2)
    near_up = shifted(piece, axis, 1)
    near_down = shifted(piece, axis, -1)
    far_up = shifted(up, axis, 1)
    far_down = shifted(down, axis, -1)
    opposite = shifted(up, axis, 2)
    return piece, near_up, up, far_up, opposite, far_down, down, near_down


def product(left_refs, right_ref, start, count):
    tiles, part, columns = right_ref.shape[1:]
    rows = pl.ds(start, count)
    total = None
    for side in range(2):
        for left_ref, tile, many in zip(left_refs[2 * side : 2 * side + 2], (0, tiles - 1), (tiles - 1, 1)):
            right = right_ref[side, pl.ds(tile, many)].reshape(many * part, columns)
            term = lax.dot_general(left_ref[:, rows], right, CONTRACT, preferred_element_type=jnp.float32)
            total = term if total is None else total + term
    return total


def place_of(offset, tiles):
    return jnp.where(offset == LAST, tiles - 1, offset - jnp.where(offset > LAST, 1, 0))


def square_kernel(place_ref, own_ref, last_ref, other_ref, other_last_ref, right_ref, out_ref, ordered_ref, staged_ref, sems):
    halves, layers, part, columns = staged_ref.shape
    tiles = right_ref.shape[0]
    z, core = place_ref[1], place_ref[2]
    way = 1 - 2 * core
    left_refs = (own_ref, last_ref, other_ref, other_last_ref)
    for tile, offset in enumerate([at for at in range(tiles) if at != LAST] + [LAST]):
        ordered_ref[0, tile] = right_ref[lax.rem(z + way * offset + tiles, tiles), core]
        ordered_ref[1, tile] = right_ref[lax.rem(z - way * offset + tiles, tiles), 1 - core]
    copies = []
    for half in range(halves):
        count = layers * part
        total = product(left_refs, ordered_ref, half * count, count)
        staged_ref[half] = total.astype(staged_ref.dtype).reshape(layers, part, columns)
        copies.append(pltpu.make_async_copy(staged_ref.at[half], out_ref.at[:, half], sems.at[half]))
        copies[-1].start()
    for copy in copies:
        copy.wait()


def filter_kernel(keep_ref, layer_ref, parts_ref, out_ref):
    layers, halves, part, columns = parts_ref.shape
    chunk = BLK // 2
    low = lax.broadcasted_iota(jnp.int32, (chunk, 2 * BLK), 1) < BLK
    for half in range(halves):
        for start in range(0, part, chunk):
            block = (half * layers * part + layer_ref[0] * part + start) // BLK
            rows = pl.ds(start, chunk)
            for lane in range(0, columns, 2 * BLK):
                lanes = pl.ds(lane, 2 * BLK)
                total = parts_ref[0, half, rows, lanes].astype(jnp.float32)
                for layer in range(1, layers):
                    total = total + parts_ref[layer, half, rows, lanes].astype(jnp.float32)
                left = keep_ref[block, lane // BLK].astype(jnp.float32)
                right = keep_ref[block, lane // BLK + 1].astype(jnp.float32)
                out_ref[half, rows, lanes] = (total * jnp.where(low, left, right)).astype(out_ref.dtype)


def cube_kernel(chosen_ref, place_ref, scale_ref, own_ref, last_ref, other_ref, other_last_ref, matrix_ref, *refs):
    pieces = refs[:8]
    out_ref, ordered_ref, total_ref, block_ref = refs[8:]
    owners, pairs, lanes = out_ref.shape
    half_blocks = matrix_ref.shape[1] // BLK
    tiles = ordered_ref.shape[1]
    row, z, core = place_ref[0], place_ref[1], place_ref[2]
    way = 1 - 2 * core
    for offset, piece in enumerate(pieces):
        distance = row + way * offset - z
        own = lax.rem(way * distance + 2 * tiles, tiles)
        other = lax.rem(tiles - own, tiles)
        ordered_ref[0, place_of(own, tiles)] = piece[core]
        ordered_ref[1, place_of(other, tiles)] = piece[1 - core]
    total_ref[...] = scale_ref[0] * matrix_ref[...].astype(jnp.float32) - 0.5 * product(
        (own_ref, last_ref, other_ref, other_last_ref), ordered_ref, 0, matrix_ref.shape[0]
    )
    low = lax.broadcasted_iota(jnp.int32, (pairs, lanes), 1) < BLK

    for owner in range(owners):
        index = chosen_ref[owner]
        live = jnp.where(index >= 0, 1.0, 0.0)
        index = jnp.maximum(index, 0)
        column = index % half_blocks
        start = pl.multiple_of(index // half_blocks * BLK, BLK)
        lane = pl.multiple_of(column // 2 * lanes, lanes)
        block = total_ref[pl.ds(start, BLK), pl.ds(lane, lanes)] * live
        turned = pltpu.roll(block, BLK, 1)
        odd = column % 2 == 1
        slot = 2 * (owner % 2)
        block_ref[slot] = jnp.where(odd, turned, block)
        block_ref[slot + 1] = jnp.where(odd, block, turned)
        even_rows = block_ref[slot, pl.ds(0, pairs, stride=2), :]
        odd_rows = block_ref[slot + 1, pl.ds(1, pairs, stride=2), :]
        out_ref[owner] = jnp.where(low, even_rows, odd_rows).astype(out_ref.dtype)


def on_device(matrix, keep_mask, send_list):
    layers = lax.axis_size("layer")
    rows_count = lax.axis_size("row")
    layer_index = lax.axis_index("layer")
    row_index = lax.axis_index("row")
    z_index = lax.axis_index("z")
    core_index = lax.axis_index("core")
    tile_rows, width = matrix.shape
    part = width // layers
    halves = tile_rows // width
    vmem = pl.BlockSpec(memory_space=pltpu.VMEM)
    smem = pl.BlockSpec(memory_space=pltpu.SMEM)
    params = pltpu.CompilerParams(vmem_limit_bytes=40 * 2**20)

    left_piece = lax.dynamic_slice_in_dim(matrix, layer_index * part, part, 1).T
    right_piece = lax.dynamic_slice_in_dim(
        matrix.reshape(halves, layers, part, width), layer_index, 1, 1
    ).reshape(halves, part, width)
    right = to_all(right_piece, "row")
    swap = [(0, 1), (1, 0)]
    pieces = ring_of_eight(left_piece, "z")
    pieces, last = pieces[:LAST] + pieces[LAST + 1 :], pieces[LAST]
    own = jnp.concatenate(pieces, axis=0)
    other = lax.ppermute(own, "core", swap)
    last, right = lax.optimization_barrier((last, right))
    left = (own, last, other, lax.ppermute(last, "core", swap))
    place = jnp.stack([row_index, z_index, core_index])

    square_part = pl.pallas_call(
        square_kernel,
        out_shape=jax.ShapeDtypeStruct((layers, halves, part, width), jnp.bfloat16),
        in_specs=[smem] + [vmem] * 5,
        out_specs=pl.BlockSpec(memory_space=pltpu.HBM),
        scratch_shapes=[
            pltpu.VMEM((halves, rows_count, part, width), jnp.bfloat16),
            pltpu.VMEM((halves, layers, part, width), jnp.bfloat16),
            pltpu.SemaphoreType.DMA((halves,)),
        ],
        compiler_params=params,
    )(place, *left, right)
    parts = lax.all_to_all(square_part, "layer", split_axis=0, concat_axis=0, tiled=True)
    filtered_piece = pl.pallas_call(
        filter_kernel,
        out_shape=jax.ShapeDtypeStruct((halves, part, width), jnp.bfloat16),
        in_specs=[smem, smem, vmem],
        out_specs=vmem,
        compiler_params=params,
    )(keep_mask, layer_index.reshape(1), parts)
    filtered = ring_of_eight(filtered_piece, "row")

    scale = jnp.where(layer_index == 0, 1.5, 0.0).astype(jnp.float32).reshape(1)
    chosen = send_list[0]
    pairs = BLK * BLK // 128
    outgoing = pl.pallas_call(
        cube_kernel,
        out_shape=jax.ShapeDtypeStruct((chosen.shape[0], pairs, 128), jnp.bfloat16),
        in_specs=[smem] * 3 + [vmem] * 13,
        out_specs=vmem,
        scratch_shapes=[
            pltpu.VMEM((halves, rows_count, part, width), jnp.bfloat16),
            pltpu.VMEM((tile_rows, width), jnp.float32),
            pltpu.VMEM((4, BLK, 128), jnp.float32),
        ],
        compiler_params=params,
    )(chosen, place, scale, *left, matrix, *filtered)
    copies = jnp.broadcast_to(outgoing[:, None], outgoing.shape[:1] + (layers,) + outgoing.shape[1:])
    copies = copies.reshape((-1,) + outgoing.shape[1:])
    everyone = lax.all_to_all(copies, ("z", "core", "layer"), split_axis=0, concat_axis=0, tiled=True)
    everyone = everyone.reshape(outgoing.shape[:1] + (layers,) + outgoing.shape[1:])
    total = everyone.astype(jnp.float32).sum(1).astype(jnp.bfloat16)
    return total.reshape(total.shape[0], BLK * BLK)


def solution(mesh):
    sizes = mesh.shape
    cores = 2
    shape = (sizes["row"], sizes["col"] // cores, cores, sizes["layer"])
    split = Mesh(mesh.devices.reshape(shape), ("row", "z", "core", "layer"))
    column = ("z", "core")
    in_specs = (P("row", column), P("row", column), P(("row",) + column, None))
    out_specs = P(("row",) + column, None)
    return jax.shard_map(
        on_device, mesh=split, in_specs=in_specs, out_specs=out_specs, check_vma=False
    )
```

```python
import jax
import jax.numpy as jnp
from jax import lax
from jax.experimental import pallas as pl
from jax.experimental.pallas import tpu as pltpu
from jax.sharding import Mesh, PartitionSpec as P

BLK = 64
CONTRACT = (((0,), (0,)), ((), ()))


def to_all(piece, axis):
    copies = jnp.broadcast_to(piece[None], (lax.axis_size(axis),) + piece.shape)
    return lax.all_to_all(copies, axis, split_axis=0, concat_axis=0, tiled=True)


def shifted(piece, axis, by):
    size = lax.axis_size(axis)
    pairs = []
    for i in range(size):
        for core, place in ((0, (i - by) % size), (1, (i + by) % size)):
            if axis == "layer":
                pairs.append((core * size + i, core * size + place))
            else:
                pairs.append((2 * i + core, 2 * place + core))
    axes = ("core", axis) if axis == "layer" else (axis, "core")
    return lax.ppermute(piece, axes, pairs)


def ring_of_eight(piece, axis):
    up = shifted(piece, axis, 2)
    down = shifted(piece, axis, -2)
    near_up = shifted(piece, axis, 1)
    near_down = shifted(piece, axis, -1)
    far_up = shifted(up, axis, 1)
    far_down = shifted(down, axis, -1)
    opposite = shifted(up, axis, 2)
    return piece, near_up, up, far_up, opposite, far_down, down, near_down


def product(own_ref, other_ref, right_ref, start, count):
    depth = own_ref.shape[0]
    columns = right_ref.shape[-1]
    rows = pl.ds(start, count)
    own = lax.dot_general(
        own_ref[:, rows], right_ref[0].reshape(depth, columns), CONTRACT, preferred_element_type=jnp.float32
    )
    other = lax.dot_general(
        other_ref[:, rows], right_ref[1].reshape(depth, columns), CONTRACT, preferred_element_type=jnp.float32
    )
    return own + other


def square_kernel(place_ref, own_ref, other_ref, right_ref, *refs):
    outs, ordered_ref, total_ref = refs[:-2], refs[-2], refs[-1]
    layers = len(outs)
    halves, part, _ = outs[0].shape
    tiles = right_ref.shape[0]
    z, core = place_ref[1], place_ref[2]
    way = 1 - 2 * core
    for offset in range(tiles):
        ordered_ref[0, offset] = right_ref[lax.rem(z + way * offset + tiles, tiles), core]
        ordered_ref[1, offset] = right_ref[lax.rem(z - way * offset + tiles, tiles), 1 - core]
    total_ref[...] = product(own_ref, other_ref, ordered_ref, 0, total_ref.shape[0])
    for offset, out_ref in enumerate(outs):
        layer = lax.rem(place_ref[3] + way * offset + layers, layers)
        for half in range(halves):
            start = pl.multiple_of((half * layers + layer) * part, part)
            out_ref[half] = total_ref[pl.ds(start, part), :].astype(out_ref.dtype)


def filter_kernel(keep_ref, place_ref, *refs):
    parts, out_ref = refs[:-1], refs[-1]
    halves, part, columns = out_ref.shape
    chunk = BLK // 2
    low = lax.broadcasted_iota(jnp.int32, (chunk, 2 * BLK), 1) < BLK
    for half in range(halves):
        for start in range(0, part, chunk):
            block = (half * columns + place_ref[3] * part + start) // BLK
            rows = pl.ds(start, chunk)
            for lane in range(0, columns, 2 * BLK):
                lanes = pl.ds(lane, 2 * BLK)
                total = parts[0][half, rows, lanes].astype(jnp.float32)
                for part_ref in parts[1:]:
                    total = total + part_ref[half, rows, lanes].astype(jnp.float32)
                left = keep_ref[block, lane // BLK].astype(jnp.float32)
                right = keep_ref[block, lane // BLK + 1].astype(jnp.float32)
                out_ref[half, rows, lanes] = (total * jnp.where(low, left, right)).astype(out_ref.dtype)


def cube_kernel(chosen_ref, place_ref, scale_ref, own_ref, other_ref, matrix_ref, *refs):
    pieces = refs[:8]
    out_ref, ordered_ref, total_ref, block_ref = refs[8:]
    owners, pairs, lanes = out_ref.shape
    half_blocks = matrix_ref.shape[1] // BLK
    tiles = ordered_ref.shape[1]
    row, z, core = place_ref[0], place_ref[1], place_ref[2]
    way = 1 - 2 * core
    for offset, piece in enumerate(pieces):
        distance = row + way * offset - z
        own = lax.rem(way * distance + 2 * tiles, tiles)
        ordered_ref[0, own] = piece[core]
        ordered_ref[1, lax.rem(tiles - own, tiles)] = piece[1 - core]
    total_ref[...] = scale_ref[0] * matrix_ref[...].astype(jnp.float32) - 0.5 * product(
        own_ref, other_ref, ordered_ref, 0, matrix_ref.shape[0]
    )
    low = lax.broadcasted_iota(jnp.int32, (pairs, lanes), 1) < BLK

    for owner in range(owners):
        index = chosen_ref[owner]
        live = jnp.where(index >= 0, 1.0, 0.0)
        index = jnp.maximum(index, 0)
        column = index % half_blocks
        start = pl.multiple_of(index // half_blocks * BLK, BLK)
        lane = pl.multiple_of(column // 2 * lanes, lanes)
        block = total_ref[pl.ds(start, BLK), pl.ds(lane, lanes)] * live
        turned = pltpu.roll(block, BLK, 1)
        odd = column % 2 == 1
        slot = 2 * (owner % 2)
        block_ref[slot] = jnp.where(odd, turned, block)
        block_ref[slot + 1] = jnp.where(odd, block, turned)
        even_rows = block_ref[slot, pl.ds(0, pairs, stride=2), :]
        odd_rows = block_ref[slot + 1, pl.ds(1, pairs, stride=2), :]
        out_ref[owner] = jnp.where(low, even_rows, odd_rows).astype(out_ref.dtype)


def on_device(matrix, keep_mask, send_list):
    layers = lax.axis_size("layer")
    rows_count = lax.axis_size("row")
    layer_index = lax.axis_index("layer")
    row_index = lax.axis_index("row")
    z_index = lax.axis_index("z")
    core_index = lax.axis_index("core")
    tile_rows, width = matrix.shape
    part = width // layers
    halves = tile_rows // width
    vmem = pl.BlockSpec(memory_space=pltpu.VMEM)
    smem = pl.BlockSpec(memory_space=pltpu.SMEM)
    params = pltpu.CompilerParams(vmem_limit_bytes=20 * 2**20)

    left_piece = lax.dynamic_slice_in_dim(matrix, layer_index * part, part, 1).T
    right_piece = lax.dynamic_slice_in_dim(
        matrix.reshape(halves, layers, part, width), layer_index, 1, 1
    ).reshape(halves, part, width)
    right = to_all(right_piece, "row")
    left_own = jnp.concatenate(ring_of_eight(left_piece, "z"), axis=0)
    left_own, right = lax.optimization_barrier((left_own, right))
    left_other = lax.ppermute(left_own, "core", [(0, 1), (1, 0)])
    place = jnp.stack([row_index, z_index, core_index, layer_index])
    ordered = pltpu.VMEM((halves, rows_count, part, width), jnp.bfloat16)
    total = pltpu.VMEM((tile_rows, width), jnp.float32)
    piece = jax.ShapeDtypeStruct((halves, part, width), jnp.bfloat16)

    mine, ahead, beyond, behind = pl.pallas_call(
        square_kernel,
        out_shape=[piece] * layers,
        in_specs=[smem] + [vmem] * 3,
        out_specs=[vmem] * layers,
        scratch_shapes=[ordered, total],
        compiler_params=params,
    )(place, left_own, left_other, right)
    passing = shifted(beyond, "layer", -1)
    from_ahead = shifted(behind, "layer", 1)
    onward = (passing.astype(jnp.float32) + ahead.astype(jnp.float32)).astype(jnp.bfloat16)
    from_behind = shifted(onward, "layer", -1)
    filtered_piece = pl.pallas_call(
        filter_kernel,
        out_shape=piece,
        in_specs=[smem] * 2 + [vmem] * 3,
        out_specs=vmem,
        compiler_params=params,
    )(keep_mask, place, mine, from_ahead, from_behind)
    filtered = ring_of_eight(filtered_piece, "row")

    scale = jnp.where(layer_index == 0, 1.5, 0.0).astype(jnp.float32).reshape(1)
    chosen = send_list[0]
    pairs = BLK * BLK // 128
    outgoing = pl.pallas_call(
        cube_kernel,
        out_shape=jax.ShapeDtypeStruct((chosen.shape[0], pairs, 128), jnp.bfloat16),
        in_specs=[smem] * 3 + [vmem] * 11,
        out_specs=vmem,
        scratch_shapes=[ordered, total, pltpu.VMEM((4, BLK, 128), jnp.float32)],
        compiler_params=params,
    )(chosen, place, scale, left_own, left_other, matrix, *filtered)
    arrived = lax.all_to_all(outgoing, ("z", "core"), split_axis=0, concat_axis=0, tiled=True)
    everyone = to_all(arrived, "layer")
    total = everyone.astype(jnp.float32).sum(0).astype(jnp.bfloat16)
    return total.reshape(total.shape[0], BLK * BLK)


def solution(mesh):
    sizes = mesh.shape
    cores = 2
    shape = (sizes["row"], sizes["col"] // cores, cores, sizes["layer"])
    split = Mesh(mesh.devices.reshape(shape), ("row", "z", "core", "layer"))
    column = ("z", "core")
    in_specs = (P("row", column), P("row", column), P(("row",) + column, None))
    out_specs = P(("row",) + column, None)
    return jax.shard_map(
        on_device, mesh=split, in_specs=in_specs, out_specs=out_specs, check_vma=False
    )
```

```python
import jax
import jax.numpy as jnp
from jax import lax
from jax.experimental import pallas as pl
from jax.experimental.pallas import tpu as pltpu
from jax.sharding import Mesh, PartitionSpec as P

BLK = 64
CONTRACT = (((0,), (0,)), ((), ()))


def to_all(piece, axis):
    copies = jnp.broadcast_to(piece[None], (lax.axis_size(axis),) + piece.shape)
    return lax.all_to_all(copies, axis, split_axis=0, concat_axis=0, tiled=True)


def shifted(piece, axis, by):
    size = lax.axis_size(axis)
    pairs = []
    for i in range(size):
        pairs.append((2 * i, 2 * ((i - by) % size)))
        pairs.append((2 * i + 1, 2 * ((i + by) % size) + 1))
    return lax.ppermute(piece, (axis, "core"), pairs)


def ring_of_eight(piece, axis):
    up = shifted(piece, axis, 2)
    down = shifted(piece, axis, -2)
    near_up = shifted(piece, axis, 1)
    near_down = shifted(piece, axis, -1)
    far_up = shifted(up, axis, 1)
    far_down = shifted(down, axis, -1)
    opposite = shifted(up, axis, 2)
    return piece, near_up, up, far_up, opposite, far_down, down, near_down


def own_kernel(place_ref, own_ref, right_ref, total_ref, ordered_ref):
    tiles, _, part, columns = right_ref.shape
    z, core = place_ref[1], place_ref[2]
    way = 1 - 2 * core
    for offset in range(tiles):
        ordered_ref[offset] = right_ref[lax.rem(z + way * offset + tiles, tiles), core]
    right = ordered_ref[...].reshape(tiles * part, columns)
    total_ref[...] = lax.dot_general(own_ref[...], right, CONTRACT, preferred_element_type=jnp.float32)


def square_kernel(place_ref, total_ref, other_ref, right_ref, out_ref, ordered_ref, staged_ref, sems):
    halves, layers, part, columns = staged_ref.shape
    tiles = right_ref.shape[0]
    z, core = place_ref[1], place_ref[2]
    way = 1 - 2 * core
    for offset in range(tiles):
        ordered_ref[offset] = right_ref[lax.rem(z - way * offset + tiles, tiles), 1 - core]
    right = ordered_ref[...].reshape(tiles * part, columns)
    copies = []
    for half in range(halves):
        rows = pl.ds(half * layers * part, layers * part)
        term = lax.dot_general(other_ref[:, rows], right, CONTRACT, preferred_element_type=jnp.float32)
        total = (total_ref[rows, :] + term).astype(staged_ref.dtype)
        staged_ref[half] = total.reshape(layers, part, columns)
        copies.append(pltpu.make_async_copy(staged_ref.at[half], out_ref.at[:, half], sems.at[half]))
        copies[-1].start()
    for copy in copies:
        copy.wait()


def turn_kernel(own_ref, other_ref, own_turned_ref, other_turned_ref):
    own_turned_ref[...] = own_ref[...].T
    other_turned_ref[...] = other_ref[...].T


def filter_kernel(keep_ref, layer_ref, parts_ref, out_ref):
    layers, halves, part, columns = parts_ref.shape
    chunk = BLK // 2
    low = lax.broadcasted_iota(jnp.int32, (chunk, 2 * BLK), 1) < BLK
    for half in range(halves):
        for start in range(0, part, chunk):
            block = (half * layers * part + layer_ref[0] * part + start) // BLK
            rows = pl.ds(start, chunk)
            for lane in range(0, columns, 2 * BLK):
                lanes = pl.ds(lane, 2 * BLK)
                total = parts_ref[0, half, rows, lanes].astype(jnp.float32)
                for layer in range(1, layers):
                    total = total + parts_ref[layer, half, rows, lanes].astype(jnp.float32)
                left = keep_ref[block, lane // BLK].astype(jnp.float32)
                right = keep_ref[block, lane // BLK + 1].astype(jnp.float32)
                out_ref[half, rows, lanes] = (total * jnp.where(low, left, right)).astype(out_ref.dtype)


def cube_kernel(chosen_ref, place_ref, scale_ref, own_ref, other_ref, matrix_ref, *refs):
    pieces = refs[:8]
    out_ref, ordered_ref, total_ref, block_ref = refs[8:]
    owners, pairs, lanes = out_ref.shape
    half_blocks = matrix_ref.shape[1] // BLK
    tiles = ordered_ref.shape[1]
    row, z, core = place_ref[0], place_ref[1], place_ref[2]
    way = 1 - 2 * core
    for offset, piece in enumerate(pieces):
        distance = row + way * offset - z
        own = lax.rem(way * distance + 2 * tiles, tiles)
        ordered_ref[0, own] = piece[core]
        ordered_ref[1, lax.rem(tiles - own, tiles)] = piece[1 - core]
    depth, columns = own_ref.shape[1], matrix_ref.shape[1]
    total_ref[...] = jnp.dot(
        own_ref[...], ordered_ref[0].reshape(depth, columns), preferred_element_type=jnp.float32
    ) + jnp.dot(
        other_ref[...], ordered_ref[1].reshape(depth, columns), preferred_element_type=jnp.float32
    )
    low = lax.broadcasted_iota(jnp.int32, (pairs, lanes), 1) < BLK

    for owner in range(owners):
        index = chosen_ref[owner]
        live = jnp.where(index >= 0, 1.0, 0.0)
        index = jnp.maximum(index, 0)
        column = index % half_blocks
        start = pl.multiple_of(index // half_blocks * BLK, BLK)
        lane = pl.multiple_of(column // 2 * lanes, lanes)
        block = matrix_ref[pl.ds(start, BLK), pl.ds(lane, lanes)].astype(jnp.float32) * scale_ref[0]
        block = (block - 0.5 * total_ref[pl.ds(start, BLK), pl.ds(lane, lanes)]) * live
        turned = pltpu.roll(block, BLK, 1)
        odd = column % 2 == 1
        slot = 2 * (owner % 2)
        block_ref[slot] = jnp.where(odd, turned, block)
        block_ref[slot + 1] = jnp.where(odd, block, turned)
        even_rows = block_ref[slot, pl.ds(0, pairs, stride=2), :]
        odd_rows = block_ref[slot + 1, pl.ds(1, pairs, stride=2), :]
        out_ref[owner] = jnp.where(low, even_rows, odd_rows).astype(out_ref.dtype)


def on_device(matrix, keep_mask, send_list):
    layers = lax.axis_size("layer")
    rows_count = lax.axis_size("row")
    layer_index = lax.axis_index("layer")
    row_index = lax.axis_index("row")
    z_index = lax.axis_index("z")
    core_index = lax.axis_index("core")
    tile_rows, width = matrix.shape
    part = width // layers
    halves = tile_rows // width
    vmem = pl.BlockSpec(memory_space=pltpu.VMEM)
    smem = pl.BlockSpec(memory_space=pltpu.SMEM)
    params = pltpu.CompilerParams(vmem_limit_bytes=40 * 2**20)

    left_piece = lax.dynamic_slice_in_dim(matrix, layer_index * part, part, 1).T
    right_piece = lax.dynamic_slice_in_dim(
        matrix.reshape(halves, layers, part, width), layer_index, 1, 1
    ).reshape(halves, part, width)
    right = to_all(right_piece, "row")
    left_own = jnp.concatenate(ring_of_eight(left_piece, "z"), axis=0)
    left_own, right = lax.optimization_barrier((left_own, right))
    left_other = lax.ppermute(left_own, "core", [(0, 1), (1, 0)])
    place = jnp.stack([row_index, z_index, core_index])

    depth = left_own.shape[0]
    ordered = pltpu.VMEM((rows_count, part, width), jnp.bfloat16)
    cost = pl.CostEstimate(
        flops=2 * tile_rows * width * depth, bytes_accessed=2 * depth * (tile_rows + width), transcendentals=0
    )
    own_total = pl.pallas_call(
        own_kernel,
        out_shape=jax.ShapeDtypeStruct((tile_rows, width), jnp.float32),
        in_specs=[smem] + [vmem] * 2,
        out_specs=vmem,
        scratch_shapes=[ordered],
        compiler_params=params,
        cost_estimate=cost,
    )(place, left_own, right)
    square_part = pl.pallas_call(
        square_kernel,
        out_shape=jax.ShapeDtypeStruct((layers, halves, part, width), jnp.bfloat16),
        in_specs=[smem] + [vmem] * 3,
        out_specs=pl.BlockSpec(memory_space=pltpu.HBM),
        scratch_shapes=[
            ordered,
            pltpu.VMEM((halves, layers, part, width), jnp.bfloat16),
            pltpu.SemaphoreType.DMA((halves,)),
        ],
        compiler_params=params,
        cost_estimate=cost,
    )(place, own_total, left_other, right)
    left_own, left_other, square_part = lax.optimization_barrier((left_own, left_other, square_part))
    turned = jax.ShapeDtypeStruct((tile_rows, depth), left_own.dtype)
    left_own, left_other = pl.pallas_call(
        turn_kernel,
        out_shape=[turned] * 2,
        in_specs=[vmem] * 2,
        out_specs=[vmem] * 2,
        compiler_params=params,
        cost_estimate=cost,
    )(left_own, left_other)
    parts = lax.all_to_all(square_part, "layer", split_axis=0, concat_axis=0, tiled=True)
    filtered_piece = pl.pallas_call(
        filter_kernel,
        out_shape=jax.ShapeDtypeStruct((halves, part, width), jnp.bfloat16),
        in_specs=[smem, smem, vmem],
        out_specs=vmem,
        compiler_params=params,
    )(keep_mask, layer_index.reshape(1), parts)
    filtered = ring_of_eight(filtered_piece, "row")

    scale = jnp.where(layer_index == 0, 1.5, 0.0).astype(jnp.float32).reshape(1)
    chosen = send_list[0]
    pairs = BLK * BLK // 128
    outgoing = pl.pallas_call(
        cube_kernel,
        out_shape=jax.ShapeDtypeStruct((chosen.shape[0], pairs, 128), jnp.bfloat16),
        in_specs=[smem] * 3 + [vmem] * 11,
        out_specs=vmem,
        scratch_shapes=[
            pltpu.VMEM((halves, rows_count, part, width), jnp.bfloat16),
            pltpu.VMEM((tile_rows, width), jnp.float32),
            pltpu.VMEM((4, BLK, 128), jnp.float32),
        ],
        compiler_params=params,
    )(chosen, place, scale, left_own, left_other, matrix, *filtered)
    arrived = lax.all_to_all(outgoing, ("z", "core"), split_axis=0, concat_axis=0, tiled=True)
    everyone = to_all(arrived, "layer")
    total = everyone.astype(jnp.float32).sum(0).astype(jnp.bfloat16)
    return total.reshape(total.shape[0], BLK * BLK)


def solution(mesh):
    sizes = mesh.shape
    cores = 2
    shape = (sizes["row"], sizes["col"] // cores, cores, sizes["layer"])
    split = Mesh(mesh.devices.reshape(shape), ("row", "z", "core", "layer"))
    column = ("z", "core")
    in_specs = (P("row", column), P("row", column), P(("row",) + column, None))
    out_specs = P(("row",) + column, None)
    return jax.shard_map(
        on_device, mesh=split, in_specs=in_specs, out_specs=out_specs, check_vma=False
    )
```

```python
import jax
import jax.numpy as jnp
from jax import lax
from jax.experimental import pallas as pl
from jax.experimental.pallas import tpu as pltpu
from jax.sharding import Mesh, PartitionSpec as P

BLK = 64
CONTRACT = (((0,), (0,)), ((), ()))


def to_all(piece, axis):
    copies = jnp.broadcast_to(piece[None], (lax.axis_size(axis),) + piece.shape)
    return lax.all_to_all(copies, axis, split_axis=0, concat_axis=0, tiled=True)


def shifted(piece, axis, by):
    size = lax.axis_size(axis)
    pairs = []
    for i in range(size):
        pairs.append((2 * i, 2 * ((i - by) % size)))
        pairs.append((2 * i + 1, 2 * ((i + by) % size) + 1))
    return lax.ppermute(piece, (axis, "core"), pairs)


def ring_of_eight(piece, axis):
    near_up = shifted(piece, axis, 1)
    near_down = shifted(piece, axis, -1)
    up = shifted(near_up, axis, 1)
    down = shifted(near_down, axis, -1)
    far_up = shifted(up, axis, 1)
    far_down = shifted(down, axis, -1)
    opposite = shifted(far_up, axis, 1)
    return piece, near_up, up, far_up, opposite, far_down, down, near_down


def own_kernel(place_ref, own_ref, right_ref, total_ref, ordered_ref):
    tiles, _, part, columns = right_ref.shape
    z, core = place_ref[1], place_ref[2]
    way = 1 - 2 * core
    for offset in range(tiles):
        ordered_ref[offset] = right_ref[lax.rem(z + way * offset + tiles, tiles), core]
    right = ordered_ref[...].reshape(tiles * part, columns)
    total_ref[...] = lax.dot_general(own_ref[...], right, CONTRACT, preferred_element_type=jnp.float32)


def square_kernel(place_ref, total_ref, other_ref, right_ref, out_ref, ordered_ref, staged_ref, sems):
    halves, layers, part, columns = staged_ref.shape
    tiles = right_ref.shape[0]
    z, core = place_ref[1], place_ref[2]
    way = 1 - 2 * core
    for offset in range(tiles):
        ordered_ref[offset] = right_ref[lax.rem(z - way * offset + tiles, tiles), 1 - core]
    right = ordered_ref[...].reshape(tiles * part, columns)
    copies = []
    for half in range(halves):
        rows = pl.ds(half * layers * part, layers * part)
        term = lax.dot_general(other_ref[:, rows], right, CONTRACT, preferred_element_type=jnp.float32)
        total = (total_ref[rows, :] + term).astype(staged_ref.dtype)
        staged_ref[half] = total.reshape(layers, part, columns)
        copies.append(pltpu.make_async_copy(staged_ref.at[half], out_ref.at[:, half], sems.at[half]))
        copies[-1].start()
    for copy in copies:
        copy.wait()


def turn_kernel(own_ref, other_ref, own_turned_ref, other_turned_ref):
    own_turned_ref[...] = own_ref[...].T
    other_turned_ref[...] = other_ref[...].T


def filter_kernel(keep_ref, layer_ref, parts_ref, out_ref):
    layers, halves, part, columns = parts_ref.shape
    chunk = BLK // 2
    low = lax.broadcasted_iota(jnp.int32, (chunk, 2 * BLK), 1) < BLK
    for half in range(halves):
        for start in range(0, part, chunk):
            block = (half * layers * part + layer_ref[0] * part + start) // BLK
            rows = pl.ds(start, chunk)
            for lane in range(0, columns, 2 * BLK):
                lanes = pl.ds(lane, 2 * BLK)
                total = parts_ref[0, half, rows, lanes].astype(jnp.float32)
                for layer in range(1, layers):
                    total = total + parts_ref[layer, half, rows, lanes].astype(jnp.float32)
                left = keep_ref[block, lane // BLK].astype(jnp.float32)
                right = keep_ref[block, lane // BLK + 1].astype(jnp.float32)
                out_ref[half, rows, lanes] = (total * jnp.where(low, left, right)).astype(out_ref.dtype)


def cube_kernel(chosen_ref, place_ref, scale_ref, own_ref, other_ref, matrix_ref, *refs):
    pieces = refs[:8]
    out_ref, ordered_ref, total_ref, block_ref = refs[8:]
    owners, pairs, lanes = out_ref.shape
    half_blocks = matrix_ref.shape[1] // BLK
    tiles = ordered_ref.shape[1]
    row, z, core = place_ref[0], place_ref[1], place_ref[2]
    way = 1 - 2 * core
    for offset, piece in enumerate(pieces):
        distance = row + way * offset - z
        own = lax.rem(way * distance + 2 * tiles, tiles)
        ordered_ref[0, own] = piece[core]
        ordered_ref[1, lax.rem(tiles - own, tiles)] = piece[1 - core]
    depth, columns = own_ref.shape[1], matrix_ref.shape[1]
    total_ref[...] = jnp.dot(
        own_ref[...], ordered_ref[0].reshape(depth, columns), preferred_element_type=jnp.float32
    ) + jnp.dot(
        other_ref[...], ordered_ref[1].reshape(depth, columns), preferred_element_type=jnp.float32
    )
    low = lax.broadcasted_iota(jnp.int32, (pairs, lanes), 1) < BLK

    for owner in range(owners):
        index = chosen_ref[owner]
        live = jnp.where(index >= 0, 1.0, 0.0)
        index = jnp.maximum(index, 0)
        column = index % half_blocks
        start = pl.multiple_of(index // half_blocks * BLK, BLK)
        lane = pl.multiple_of(column // 2 * lanes, lanes)
        block = matrix_ref[pl.ds(start, BLK), pl.ds(lane, lanes)].astype(jnp.float32) * scale_ref[0]
        block = (block - 0.5 * total_ref[pl.ds(start, BLK), pl.ds(lane, lanes)]) * live
        turned = pltpu.roll(block, BLK, 1)
        odd = column % 2 == 1
        slot = 2 * (owner % 2)
        block_ref[slot] = jnp.where(odd, turned, block)
        block_ref[slot + 1] = jnp.where(odd, block, turned)
        even_rows = block_ref[slot, pl.ds(0, pairs, stride=2), :]
        odd_rows = block_ref[slot + 1, pl.ds(1, pairs, stride=2), :]
        out_ref[owner] = jnp.where(low, even_rows, odd_rows).astype(out_ref.dtype)


def on_device(matrix, keep_mask, send_list):
    layers = lax.axis_size("layer")
    rows_count = lax.axis_size("row")
    layer_index = lax.axis_index("layer")
    row_index = lax.axis_index("row")
    z_index = lax.axis_index("z")
    core_index = lax.axis_index("core")
    tile_rows, width = matrix.shape
    part = width // layers
    halves = tile_rows // width
    vmem = pl.BlockSpec(memory_space=pltpu.VMEM)
    smem = pl.BlockSpec(memory_space=pltpu.SMEM)
    params = pltpu.CompilerParams(vmem_limit_bytes=40 * 2**20)

    left_piece = lax.dynamic_slice_in_dim(matrix, layer_index * part, part, 1).T
    right_piece = lax.dynamic_slice_in_dim(
        matrix.reshape(halves, layers, part, width), layer_index, 1, 1
    ).reshape(halves, part, width)
    right = to_all(right_piece, "row")
    left_own = jnp.concatenate(ring_of_eight(left_piece, "z"), axis=0)
    left_own, right = lax.optimization_barrier((left_own, right))
    left_other = lax.ppermute(left_own, "core", [(0, 1), (1, 0)])
    place = jnp.stack([row_index, z_index, core_index])

    depth = left_own.shape[0]
    ordered = pltpu.VMEM((rows_count, part, width), jnp.bfloat16)
    cost = pl.CostEstimate(
        flops=2 * tile_rows * width * depth, bytes_accessed=2 * depth * (tile_rows + width), transcendentals=0
    )
    own_total = pl.pallas_call(
        own_kernel,
        out_shape=jax.ShapeDtypeStruct((tile_rows, width), jnp.float32),
        in_specs=[smem] + [vmem] * 2,
        out_specs=vmem,
        scratch_shapes=[ordered],
        compiler_params=params,
        cost_estimate=cost,
    )(place, left_own, right)
    square_part = pl.pallas_call(
        square_kernel,
        out_shape=jax.ShapeDtypeStruct((layers, halves, part, width), jnp.bfloat16),
        in_specs=[smem] + [vmem] * 3,
        out_specs=pl.BlockSpec(memory_space=pltpu.HBM),
        scratch_shapes=[
            ordered,
            pltpu.VMEM((halves, layers, part, width), jnp.bfloat16),
            pltpu.SemaphoreType.DMA((halves,)),
        ],
        compiler_params=params,
        cost_estimate=cost,
    )(place, own_total, left_other, right)
    left_own, left_other, square_part = lax.optimization_barrier((left_own, left_other, square_part))
    turned = jax.ShapeDtypeStruct((tile_rows, depth), left_own.dtype)
    left_own, left_other = pl.pallas_call(
        turn_kernel,
        out_shape=[turned] * 2,
        in_specs=[vmem] * 2,
        out_specs=[vmem] * 2,
        compiler_params=params,
        cost_estimate=cost,
    )(left_own, left_other)
    parts = lax.all_to_all(square_part, "layer", split_axis=0, concat_axis=0, tiled=True)
    filtered_piece = pl.pallas_call(
        filter_kernel,
        out_shape=jax.ShapeDtypeStruct((halves, part, width), jnp.bfloat16),
        in_specs=[smem, smem, vmem],
        out_specs=vmem,
        compiler_params=params,
    )(keep_mask, layer_index.reshape(1), parts)
    filtered = ring_of_eight(filtered_piece, "row")

    scale = jnp.where(layer_index == 0, 1.5, 0.0).astype(jnp.float32).reshape(1)
    chosen = send_list[0]
    pairs = BLK * BLK // 128
    outgoing = pl.pallas_call(
        cube_kernel,
        out_shape=jax.ShapeDtypeStruct((chosen.shape[0], pairs, 128), jnp.bfloat16),
        in_specs=[smem] * 3 + [vmem] * 11,
        out_specs=vmem,
        scratch_shapes=[
            pltpu.VMEM((halves, rows_count, part, width), jnp.bfloat16),
            pltpu.VMEM((tile_rows, width), jnp.float32),
            pltpu.VMEM((4, BLK, 128), jnp.float32),
        ],
        compiler_params=params,
    )(chosen, place, scale, left_own, left_other, matrix, *filtered)
    arrived = lax.all_to_all(outgoing, ("z", "core"), split_axis=0, concat_axis=0, tiled=True)
    everyone = to_all(arrived, "layer")
    total = everyone.astype(jnp.float32).sum(0).astype(jnp.bfloat16)
    return total.reshape(total.shape[0], BLK * BLK)


def solution(mesh):
    sizes = mesh.shape
    cores = 2
    shape = (sizes["row"], sizes["col"] // cores, cores, sizes["layer"])
    split = Mesh(mesh.devices.reshape(shape), ("row", "z", "core", "layer"))
    column = ("z", "core")
    in_specs = (P("row", column), P("row", column), P(("row",) + column, None))
    out_specs = P(("row",) + column, None)
    return jax.shard_map(
        on_device, mesh=split, in_specs=in_specs, out_specs=out_specs, check_vma=False
    )
```

```python
import jax
import jax.numpy as jnp
from jax import lax
from jax.experimental import pallas as pl
from jax.experimental.pallas import tpu as pltpu
from jax.sharding import Mesh, PartitionSpec as P

BLK = 64
CONTRACT = (((0,), (0,)), ((), ()))


def to_all(piece, axis):
    copies = jnp.broadcast_to(piece[None], (lax.axis_size(axis),) + piece.shape)
    return lax.all_to_all(copies, axis, split_axis=0, concat_axis=0, tiled=True)


def shifted(piece, axis, by):
    size = lax.axis_size(axis)
    pairs = []
    for i in range(size):
        pairs.append((2 * i, 2 * ((i - by) % size)))
        pairs.append((2 * i + 1, 2 * ((i + by) % size) + 1))
    return lax.ppermute(piece, (axis, "core"), pairs)


def ring_of_eight(piece, axis):
    up = shifted(piece, axis, 2)
    down = shifted(piece, axis, -2)
    near_up = shifted(piece, axis, 1)
    near_down = shifted(piece, axis, -1)
    far_up = shifted(piece, axis, 3)
    far_down = shifted(piece, axis, -3)
    opposite = shifted(up, axis, 2)
    return piece, near_up, up, far_up, opposite, far_down, down, near_down


def own_kernel(place_ref, own_ref, right_ref, total_ref, ordered_ref):
    tiles, _, part, columns = right_ref.shape
    z, core = place_ref[1], place_ref[2]
    way = 1 - 2 * core
    for offset in range(tiles):
        ordered_ref[offset] = right_ref[lax.rem(z + way * offset + tiles, tiles), core]
    right = ordered_ref[...].reshape(tiles * part, columns)
    total_ref[...] = lax.dot_general(own_ref[...], right, CONTRACT, preferred_element_type=jnp.float32)


def square_kernel(place_ref, total_ref, other_ref, right_ref, out_ref, ordered_ref, staged_ref, sems):
    halves, layers, part, columns = staged_ref.shape
    tiles = right_ref.shape[0]
    z, core = place_ref[1], place_ref[2]
    way = 1 - 2 * core
    for offset in range(tiles):
        ordered_ref[offset] = right_ref[lax.rem(z - way * offset + tiles, tiles), 1 - core]
    right = ordered_ref[...].reshape(tiles * part, columns)
    copies = []
    for half in range(halves):
        rows = pl.ds(half * layers * part, layers * part)
        term = lax.dot_general(other_ref[:, rows], right, CONTRACT, preferred_element_type=jnp.float32)
        total = (total_ref[rows, :] + term).astype(staged_ref.dtype)
        staged_ref[half] = total.reshape(layers, part, columns)
        copies.append(pltpu.make_async_copy(staged_ref.at[half], out_ref.at[:, half], sems.at[half]))
        copies[-1].start()
    for copy in copies:
        copy.wait()


def turn_kernel(own_ref, other_ref, own_turned_ref, other_turned_ref):
    own_turned_ref[...] = own_ref[...].T
    other_turned_ref[...] = other_ref[...].T


def filter_kernel(keep_ref, layer_ref, parts_ref, out_ref):
    layers, halves, part, columns = parts_ref.shape
    chunk = BLK // 2
    low = lax.broadcasted_iota(jnp.int32, (chunk, 2 * BLK), 1) < BLK
    for half in range(halves):
        for start in range(0, part, chunk):
            block = (half * layers * part + layer_ref[0] * part + start) // BLK
            rows = pl.ds(start, chunk)
            for lane in range(0, columns, 2 * BLK):
                lanes = pl.ds(lane, 2 * BLK)
                total = parts_ref[0, half, rows, lanes].astype(jnp.float32)
                for layer in range(1, layers):
                    total = total + parts_ref[layer, half, rows, lanes].astype(jnp.float32)
                left = keep_ref[block, lane // BLK].astype(jnp.float32)
                right = keep_ref[block, lane // BLK + 1].astype(jnp.float32)
                out_ref[half, rows, lanes] = (total * jnp.where(low, left, right)).astype(out_ref.dtype)


def cube_kernel(chosen_ref, place_ref, scale_ref, own_ref, other_ref, matrix_ref, *refs):
    pieces = refs[:8]
    out_ref, ordered_ref, total_ref, block_ref = refs[8:]
    owners, pairs, lanes = out_ref.shape
    half_blocks = matrix_ref.shape[1] // BLK
    tiles = ordered_ref.shape[1]
    row, z, core = place_ref[0], place_ref[1], place_ref[2]
    way = 1 - 2 * core
    for offset, piece in enumerate(pieces):
        distance = row + way * offset - z
        own = lax.rem(way * distance + 2 * tiles, tiles)
        ordered_ref[0, own] = piece[core]
        ordered_ref[1, lax.rem(tiles - own, tiles)] = piece[1 - core]
    depth, columns = own_ref.shape[1], matrix_ref.shape[1]
    total_ref[...] = jnp.dot(
        own_ref[...], ordered_ref[0].reshape(depth, columns), preferred_element_type=jnp.float32
    ) + jnp.dot(
        other_ref[...], ordered_ref[1].reshape(depth, columns), preferred_element_type=jnp.float32
    )
    low = lax.broadcasted_iota(jnp.int32, (pairs, lanes), 1) < BLK

    for owner in range(owners):
        index = chosen_ref[owner]
        live = jnp.where(index >= 0, 1.0, 0.0)
        index = jnp.maximum(index, 0)
        column = index % half_blocks
        start = pl.multiple_of(index // half_blocks * BLK, BLK)
        lane = pl.multiple_of(column // 2 * lanes, lanes)
        block = matrix_ref[pl.ds(start, BLK), pl.ds(lane, lanes)].astype(jnp.float32) * scale_ref[0]
        block = (block - 0.5 * total_ref[pl.ds(start, BLK), pl.ds(lane, lanes)]) * live
        turned = pltpu.roll(block, BLK, 1)
        odd = column % 2 == 1
        slot = 2 * (owner % 2)
        block_ref[slot] = jnp.where(odd, turned, block)
        block_ref[slot + 1] = jnp.where(odd, block, turned)
        even_rows = block_ref[slot, pl.ds(0, pairs, stride=2), :]
        odd_rows = block_ref[slot + 1, pl.ds(1, pairs, stride=2), :]
        out_ref[owner] = jnp.where(low, even_rows, odd_rows).astype(out_ref.dtype)


def on_device(matrix, keep_mask, send_list):
    layers = lax.axis_size("layer")
    rows_count = lax.axis_size("row")
    layer_index = lax.axis_index("layer")
    row_index = lax.axis_index("row")
    z_index = lax.axis_index("z")
    core_index = lax.axis_index("core")
    tile_rows, width = matrix.shape
    part = width // layers
    halves = tile_rows // width
    vmem = pl.BlockSpec(memory_space=pltpu.VMEM)
    smem = pl.BlockSpec(memory_space=pltpu.SMEM)
    params = pltpu.CompilerParams(vmem_limit_bytes=40 * 2**20)

    left_piece = lax.dynamic_slice_in_dim(matrix, layer_index * part, part, 1).T
    right_piece = lax.dynamic_slice_in_dim(
        matrix.reshape(halves, layers, part, width), layer_index, 1, 1
    ).reshape(halves, part, width)
    right = to_all(right_piece, "row")
    left_own = jnp.concatenate(ring_of_eight(left_piece, "z"), axis=0)
    left_own, right = lax.optimization_barrier((left_own, right))
    left_other = lax.ppermute(left_own, "core", [(0, 1), (1, 0)])
    place = jnp.stack([row_index, z_index, core_index])

    depth = left_own.shape[0]
    ordered = pltpu.VMEM((rows_count, part, width), jnp.bfloat16)
    cost = pl.CostEstimate(
        flops=2 * tile_rows * width * depth, bytes_accessed=2 * depth * (tile_rows + width), transcendentals=0
    )
    own_total = pl.pallas_call(
        own_kernel,
        out_shape=jax.ShapeDtypeStruct((tile_rows, width), jnp.float32),
        in_specs=[smem] + [vmem] * 2,
        out_specs=vmem,
        scratch_shapes=[ordered],
        compiler_params=params,
        cost_estimate=cost,
    )(place, left_own, right)
    square_part = pl.pallas_call(
        square_kernel,
        out_shape=jax.ShapeDtypeStruct((layers, halves, part, width), jnp.bfloat16),
        in_specs=[smem] + [vmem] * 3,
        out_specs=pl.BlockSpec(memory_space=pltpu.HBM),
        scratch_shapes=[
            ordered,
            pltpu.VMEM((halves, layers, part, width), jnp.bfloat16),
            pltpu.SemaphoreType.DMA((halves,)),
        ],
        compiler_params=params,
        cost_estimate=cost,
    )(place, own_total, left_other, right)
    left_own, left_other, square_part = lax.optimization_barrier((left_own, left_other, square_part))
    turned = jax.ShapeDtypeStruct((tile_rows, depth), left_own.dtype)
    left_own, left_other = pl.pallas_call(
        turn_kernel,
        out_shape=[turned] * 2,
        in_specs=[vmem] * 2,
        out_specs=[vmem] * 2,
        compiler_params=params,
        cost_estimate=cost,
    )(left_own, left_other)
    parts = lax.all_to_all(square_part, "layer", split_axis=0, concat_axis=0, tiled=True)
    filtered_piece = pl.pallas_call(
        filter_kernel,
        out_shape=jax.ShapeDtypeStruct((halves, part, width), jnp.bfloat16),
        in_specs=[smem, smem, vmem],
        out_specs=vmem,
        compiler_params=params,
    )(keep_mask, layer_index.reshape(1), parts)
    filtered = ring_of_eight(filtered_piece, "row")

    scale = jnp.where(layer_index == 0, 1.5, 0.0).astype(jnp.float32).reshape(1)
    chosen = send_list[0]
    pairs = BLK * BLK // 128
    outgoing = pl.pallas_call(
        cube_kernel,
        out_shape=jax.ShapeDtypeStruct((chosen.shape[0], pairs, 128), jnp.bfloat16),
        in_specs=[smem] * 3 + [vmem] * 11,
        out_specs=vmem,
        scratch_shapes=[
            pltpu.VMEM((halves, rows_count, part, width), jnp.bfloat16),
            pltpu.VMEM((tile_rows, width), jnp.float32),
            pltpu.VMEM((4, BLK, 128), jnp.float32),
        ],
        compiler_params=params,
    )(chosen, place, scale, left_own, left_other, matrix, *filtered)
    arrived = lax.all_to_all(outgoing, ("z", "core"), split_axis=0, concat_axis=0, tiled=True)
    everyone = to_all(arrived, "layer")
    total = everyone.astype(jnp.float32).sum(0).astype(jnp.bfloat16)
    return total.reshape(total.shape[0], BLK * BLK)


def solution(mesh):
    sizes = mesh.shape
    cores = 2
    shape = (sizes["row"], sizes["col"] // cores, cores, sizes["layer"])
    split = Mesh(mesh.devices.reshape(shape), ("row", "z", "core", "layer"))
    column = ("z", "core")
    in_specs = (P("row", column), P("row", column), P(("row",) + column, None))
    out_specs = P(("row",) + column, None)
    return jax.shard_map(
        on_device, mesh=split, in_specs=in_specs, out_specs=out_specs, check_vma=False
    )
```

```python
import jax
import jax.numpy as jnp
from jax import lax
from jax.experimental import pallas as pl
from jax.experimental.pallas import tpu as pltpu
from jax.sharding import Mesh, PartitionSpec as P

BLK = 64
CONTRACT = (((0,), (0,)), ((), ()))


def to_all(piece, axis):
    copies = jnp.broadcast_to(piece[None], (lax.axis_size(axis),) + piece.shape)
    return lax.all_to_all(copies, axis, split_axis=0, concat_axis=0, tiled=True)


def shifted(piece, axis, by):
    size = lax.axis_size(axis)
    pairs = []
    for i in range(size):
        pairs.append((2 * i, 2 * ((i - by) % size)))
        pairs.append((2 * i + 1, 2 * ((i + by) % size) + 1))
    return lax.ppermute(piece, (axis, "core"), pairs)


def ring_of_eight(piece, axis, near_last=False):
    up = shifted(piece, axis, 2)
    down = shifted(piece, axis, -2)
    late = piece
    if near_last:
        late, up = lax.optimization_barrier((piece, up))
    opposite = shifted(up, axis, 2)
    far_up = shifted(up, axis, 1)
    far_down = shifted(down, axis, -1)
    near_up = shifted(late, axis, 1)
    near_down = shifted(late, axis, -1)
    return piece, near_up, up, far_up, opposite, far_down, down, near_down


def own_kernel(place_ref, own_ref, right_ref, total_ref, ordered_ref):
    tiles, _, part, columns = right_ref.shape
    z, core = place_ref[1], place_ref[2]
    way = 1 - 2 * core
    for offset in range(tiles):
        ordered_ref[offset] = right_ref[lax.rem(z + way * offset + tiles, tiles), core]
    right = ordered_ref[...].reshape(tiles * part, columns)
    total_ref[...] = lax.dot_general(own_ref[...], right, CONTRACT, preferred_element_type=jnp.float32)


def square_kernel(place_ref, total_ref, other_ref, right_ref, out_ref, ordered_ref, staged_ref, sems):
    halves, layers, part, columns = staged_ref.shape
    tiles = right_ref.shape[0]
    z, core = place_ref[1], place_ref[2]
    way = 1 - 2 * core
    for offset in range(tiles):
        ordered_ref[offset] = right_ref[lax.rem(z - way * offset + tiles, tiles), 1 - core]
    right = ordered_ref[...].reshape(tiles * part, columns)
    copies = []
    for half in range(halves):
        rows = pl.ds(half * layers * part, layers * part)
        term = lax.dot_general(other_ref[:, rows], right, CONTRACT, preferred_element_type=jnp.float32)
        total = (total_ref[rows, :] + term).astype(staged_ref.dtype)
        staged_ref[half] = total.reshape(layers, part, columns)
        copies.append(pltpu.make_async_copy(staged_ref.at[half], out_ref.at[:, half], sems.at[half]))
        copies[-1].start()
    for copy in copies:
        copy.wait()


def turn_kernel(own_ref, other_ref, own_turned_ref, other_turned_ref):
    own_turned_ref[...] = own_ref[...].T
    other_turned_ref[...] = other_ref[...].T


def filter_kernel(keep_ref, layer_ref, parts_ref, out_ref):
    layers, halves, part, columns = parts_ref.shape
    chunk = BLK // 2
    low = lax.broadcasted_iota(jnp.int32, (chunk, 2 * BLK), 1) < BLK
    for half in range(halves):
        for start in range(0, part, chunk):
            block = (half * layers * part + layer_ref[0] * part + start) // BLK
            rows = pl.ds(start, chunk)
            for lane in range(0, columns, 2 * BLK):
                lanes = pl.ds(lane, 2 * BLK)
                total = parts_ref[0, half, rows, lanes].astype(jnp.float32)
                for layer in range(1, layers):
                    total = total + parts_ref[layer, half, rows, lanes].astype(jnp.float32)
                left = keep_ref[block, lane // BLK].astype(jnp.float32)
                right = keep_ref[block, lane // BLK + 1].astype(jnp.float32)
                out_ref[half, rows, lanes] = (total * jnp.where(low, left, right)).astype(out_ref.dtype)


def cube_kernel(chosen_ref, place_ref, scale_ref, own_ref, other_ref, matrix_ref, *refs):
    pieces = refs[:8]
    out_ref, ordered_ref, total_ref, block_ref = refs[8:]
    owners, pairs, lanes = out_ref.shape
    half_blocks = matrix_ref.shape[1] // BLK
    tiles = ordered_ref.shape[1]
    row, z, core = place_ref[0], place_ref[1], place_ref[2]
    way = 1 - 2 * core
    for offset, piece in enumerate(pieces):
        distance = row + way * offset - z
        own = lax.rem(way * distance + 2 * tiles, tiles)
        ordered_ref[0, own] = piece[core]
        ordered_ref[1, lax.rem(tiles - own, tiles)] = piece[1 - core]
    depth, columns = own_ref.shape[1], matrix_ref.shape[1]
    total_ref[...] = jnp.dot(
        own_ref[...], ordered_ref[0].reshape(depth, columns), preferred_element_type=jnp.float32
    ) + jnp.dot(
        other_ref[...], ordered_ref[1].reshape(depth, columns), preferred_element_type=jnp.float32
    )
    low = lax.broadcasted_iota(jnp.int32, (pairs, lanes), 1) < BLK

    for owner in range(owners):
        index = chosen_ref[owner]
        live = jnp.where(index >= 0, 1.0, 0.0)
        index = jnp.maximum(index, 0)
        column = index % half_blocks
        start = pl.multiple_of(index // half_blocks * BLK, BLK)
        lane = pl.multiple_of(column // 2 * lanes, lanes)
        block = matrix_ref[pl.ds(start, BLK), pl.ds(lane, lanes)].astype(jnp.float32) * scale_ref[0]
        block = (block - 0.5 * total_ref[pl.ds(start, BLK), pl.ds(lane, lanes)]) * live
        turned = pltpu.roll(block, BLK, 1)
        odd = column % 2 == 1
        slot = 2 * (owner % 2)
        block_ref[slot] = jnp.where(odd, turned, block)
        block_ref[slot + 1] = jnp.where(odd, block, turned)
        even_rows = block_ref[slot, pl.ds(0, pairs, stride=2), :]
        odd_rows = block_ref[slot + 1, pl.ds(1, pairs, stride=2), :]
        out_ref[owner] = jnp.where(low, even_rows, odd_rows).astype(out_ref.dtype)


def on_device(matrix, keep_mask, send_list):
    layers = lax.axis_size("layer")
    rows_count = lax.axis_size("row")
    layer_index = lax.axis_index("layer")
    row_index = lax.axis_index("row")
    z_index = lax.axis_index("z")
    core_index = lax.axis_index("core")
    tile_rows, width = matrix.shape
    part = width // layers
    halves = tile_rows // width
    vmem = pl.BlockSpec(memory_space=pltpu.VMEM)
    smem = pl.BlockSpec(memory_space=pltpu.SMEM)
    params = pltpu.CompilerParams(vmem_limit_bytes=40 * 2**20)

    left_piece = lax.dynamic_slice_in_dim(matrix, layer_index * part, part, 1).T
    right_piece = lax.dynamic_slice_in_dim(
        matrix.reshape(halves, layers, part, width), layer_index, 1, 1
    ).reshape(halves, part, width)
    right = to_all(right_piece, "row")
    left_own = jnp.concatenate(ring_of_eight(left_piece, "z"), axis=0)
    left_own, right = lax.optimization_barrier((left_own, right))
    left_other = lax.ppermute(left_own, "core", [(0, 1), (1, 0)])
    place = jnp.stack([row_index, z_index, core_index])

    depth = left_own.shape[0]
    ordered = pltpu.VMEM((rows_count, part, width), jnp.bfloat16)
    cost = pl.CostEstimate(
        flops=2 * tile_rows * width * depth, bytes_accessed=2 * depth * (tile_rows + width), transcendentals=0
    )
    own_total = pl.pallas_call(
        own_kernel,
        out_shape=jax.ShapeDtypeStruct((tile_rows, width), jnp.float32),
        in_specs=[smem] + [vmem] * 2,
        out_specs=vmem,
        scratch_shapes=[ordered],
        compiler_params=params,
        cost_estimate=cost,
    )(place, left_own, right)
    square_part = pl.pallas_call(
        square_kernel,
        out_shape=jax.ShapeDtypeStruct((layers, halves, part, width), jnp.bfloat16),
        in_specs=[smem] + [vmem] * 3,
        out_specs=pl.BlockSpec(memory_space=pltpu.HBM),
        scratch_shapes=[
            ordered,
            pltpu.VMEM((halves, layers, part, width), jnp.bfloat16),
            pltpu.SemaphoreType.DMA((halves,)),
        ],
        compiler_params=params,
        cost_estimate=cost,
    )(place, own_total, left_other, right)
    left_own, left_other, square_part = lax.optimization_barrier((left_own, left_other, square_part))
    turned = jax.ShapeDtypeStruct((tile_rows, depth), left_own.dtype)
    left_own, left_other = pl.pallas_call(
        turn_kernel,
        out_shape=[turned] * 2,
        in_specs=[vmem] * 2,
        out_specs=[vmem] * 2,
        compiler_params=params,
        cost_estimate=cost,
    )(left_own, left_other)
    parts = lax.all_to_all(square_part, "layer", split_axis=0, concat_axis=0, tiled=True)
    filtered_piece = pl.pallas_call(
        filter_kernel,
        out_shape=jax.ShapeDtypeStruct((halves, part, width), jnp.bfloat16),
        in_specs=[smem, smem, vmem],
        out_specs=vmem,
        compiler_params=params,
    )(keep_mask, layer_index.reshape(1), parts)
    filtered = ring_of_eight(filtered_piece, "row", near_last=True)

    scale = jnp.where(layer_index == 0, 1.5, 0.0).astype(jnp.float32).reshape(1)
    chosen = send_list[0]
    pairs = BLK * BLK // 128
    outgoing = pl.pallas_call(
        cube_kernel,
        out_shape=jax.ShapeDtypeStruct((chosen.shape[0], pairs, 128), jnp.bfloat16),
        in_specs=[smem] * 3 + [vmem] * 11,
        out_specs=vmem,
        scratch_shapes=[
            pltpu.VMEM((halves, rows_count, part, width), jnp.bfloat16),
            pltpu.VMEM((tile_rows, width), jnp.float32),
            pltpu.VMEM((4, BLK, 128), jnp.float32),
        ],
        compiler_params=params,
    )(chosen, place, scale, left_own, left_other, matrix, *filtered)
    arrived = lax.all_to_all(outgoing, ("z", "core"), split_axis=0, concat_axis=0, tiled=True)
    everyone = to_all(arrived, "layer")
    total = everyone.astype(jnp.float32).sum(0).astype(jnp.bfloat16)
    return total.reshape(total.shape[0], BLK * BLK)


def solution(mesh):
    sizes = mesh.shape
    cores = 2
    shape = (sizes["row"], sizes["col"] // cores, cores, sizes["layer"])
    split = Mesh(mesh.devices.reshape(shape), ("row", "z", "core", "layer"))
    column = ("z", "core")
    in_specs = (P("row", column), P("row", column), P(("row",) + column, None))
    out_specs = P(("row",) + column, None)
    return jax.shard_map(
        on_device, mesh=split, in_specs=in_specs, out_specs=out_specs, check_vma=False
    )
```

```python
import jax
import jax.numpy as jnp
from jax import lax
from jax.experimental import pallas as pl
from jax.experimental.pallas import tpu as pltpu
from jax.sharding import Mesh, PartitionSpec as P

BLK = 64
CONTRACT = (((0,), (0,)), ((), ()))


def to_all(piece, axis):
    copies = jnp.broadcast_to(piece[None], (lax.axis_size(axis),) + piece.shape)
    return lax.all_to_all(copies, axis, split_axis=0, concat_axis=0, tiled=True)


def shifted(piece, axis, by):
    size = lax.axis_size(axis)
    pairs = []
    for i in range(size):
        pairs.append((2 * i, 2 * ((i - by) % size)))
        pairs.append((2 * i + 1, 2 * ((i + by) % size) + 1))
    return lax.ppermute(piece, (axis, "core"), pairs)


def ring_of_eight(piece, axis):
    up = shifted(piece, axis, 2)
    down = shifted(piece, axis, -2)
    near_up = shifted(piece, axis, 1)
    near_down = shifted(piece, axis, -1)
    far_up = shifted(up, axis, 1)
    far_down = shifted(down, axis, -1)
    opposite = shifted(up, axis, 2)
    return piece, near_up, up, far_up, opposite, far_down, down, near_down


def ring_with_pair(piece, axis):
    up = shifted(piece, axis, 2)
    down = shifted(piece, axis, -2)
    near_up = shifted(piece, axis, 1)
    near_down = shifted(piece, axis, -1)
    pair = shifted(jnp.concatenate([near_up, up]), axis, 2)
    far_down = shifted(down, axis, -1)
    return piece, near_up, up, pair, far_down, down, near_down


def own_kernel(place_ref, own_ref, right_ref, total_ref, ordered_ref):
    tiles, _, part, columns = right_ref.shape
    z, core = place_ref[1], place_ref[2]
    way = 1 - 2 * core
    for offset in range(tiles):
        ordered_ref[offset] = right_ref[lax.rem(z + way * offset + tiles, tiles), core]
    right = ordered_ref[...].reshape(tiles * part, columns)
    total_ref[...] = lax.dot_general(own_ref[...], right, CONTRACT, preferred_element_type=jnp.float32)


def square_kernel(place_ref, total_ref, other_ref, right_ref, out_ref, ordered_ref, staged_ref, sems):
    halves, layers, part, columns = staged_ref.shape
    tiles = right_ref.shape[0]
    z, core = place_ref[1], place_ref[2]
    way = 1 - 2 * core
    for offset in range(tiles):
        ordered_ref[offset] = right_ref[lax.rem(z - way * offset + tiles, tiles), 1 - core]
    right = ordered_ref[...].reshape(tiles * part, columns)
    copies = []
    for half in range(halves):
        rows = pl.ds(half * layers * part, layers * part)
        term = lax.dot_general(other_ref[:, rows], right, CONTRACT, preferred_element_type=jnp.float32)
        total = (total_ref[rows, :] + term).astype(staged_ref.dtype)
        staged_ref[half] = total.reshape(layers, part, columns)
        copies.append(pltpu.make_async_copy(staged_ref.at[half], out_ref.at[:, half], sems.at[half]))
        copies[-1].start()
    for copy in copies:
        copy.wait()


def turn_kernel(own_ref, other_ref, own_turned_ref, other_turned_ref):
    own_turned_ref[...] = own_ref[...].T
    other_turned_ref[...] = other_ref[...].T


def filter_kernel(keep_ref, layer_ref, parts_ref, out_ref):
    layers, halves, part, columns = parts_ref.shape
    chunk = BLK // 2
    low = lax.broadcasted_iota(jnp.int32, (chunk, 2 * BLK), 1) < BLK
    for half in range(halves):
        for start in range(0, part, chunk):
            block = (half * layers * part + layer_ref[0] * part + start) // BLK
            rows = pl.ds(start, chunk)
            for lane in range(0, columns, 2 * BLK):
                lanes = pl.ds(lane, 2 * BLK)
                total = parts_ref[0, half, rows, lanes].astype(jnp.float32)
                for layer in range(1, layers):
                    total = total + parts_ref[layer, half, rows, lanes].astype(jnp.float32)
                left = keep_ref[block, lane // BLK].astype(jnp.float32)
                right = keep_ref[block, lane // BLK + 1].astype(jnp.float32)
                out_ref[half, rows, lanes] = (total * jnp.where(low, left, right)).astype(out_ref.dtype)


def cube_kernel(chosen_ref, place_ref, scale_ref, own_ref, other_ref, matrix_ref, *refs):
    halves = refs[0].shape[0]
    pair = (refs[3].at[pl.ds(0, halves)], refs[3].at[pl.ds(halves, halves)])
    pieces = refs[:3] + pair + refs[4:7]
    out_ref, ordered_ref, total_ref, block_ref = refs[7:]
    owners, pairs, lanes = out_ref.shape
    half_blocks = matrix_ref.shape[1] // BLK
    tiles = ordered_ref.shape[1]
    row, z, core = place_ref[0], place_ref[1], place_ref[2]
    way = 1 - 2 * core
    for offset, piece in enumerate(pieces):
        distance = row + way * offset - z
        own = lax.rem(way * distance + 2 * tiles, tiles)
        ordered_ref[0, own] = piece[core]
        ordered_ref[1, lax.rem(tiles - own, tiles)] = piece[1 - core]
    depth, columns = own_ref.shape[1], matrix_ref.shape[1]
    total_ref[...] = jnp.dot(
        own_ref[...], ordered_ref[0].reshape(depth, columns), preferred_element_type=jnp.float32
    ) + jnp.dot(
        other_ref[...], ordered_ref[1].reshape(depth, columns), preferred_element_type=jnp.float32
    )
    low = lax.broadcasted_iota(jnp.int32, (pairs, lanes), 1) < BLK

    for owner in range(owners):
        index = chosen_ref[owner]
        live = jnp.where(index >= 0, 1.0, 0.0)
        index = jnp.maximum(index, 0)
        column = index % half_blocks
        start = pl.multiple_of(index // half_blocks * BLK, BLK)
        lane = pl.multiple_of(column // 2 * lanes, lanes)
        block = matrix_ref[pl.ds(start, BLK), pl.ds(lane, lanes)].astype(jnp.float32) * scale_ref[0]
        block = (block - 0.5 * total_ref[pl.ds(start, BLK), pl.ds(lane, lanes)]) * live
        turned = pltpu.roll(block, BLK, 1)
        odd = column % 2 == 1
        slot = 2 * (owner % 2)
        block_ref[slot] = jnp.where(odd, turned, block)
        block_ref[slot + 1] = jnp.where(odd, block, turned)
        even_rows = block_ref[slot, pl.ds(0, pairs, stride=2), :]
        odd_rows = block_ref[slot + 1, pl.ds(1, pairs, stride=2), :]
        out_ref[owner] = jnp.where(low, even_rows, odd_rows).astype(out_ref.dtype)


def on_device(matrix, keep_mask, send_list):
    layers = lax.axis_size("layer")
    rows_count = lax.axis_size("row")
    layer_index = lax.axis_index("layer")
    row_index = lax.axis_index("row")
    z_index = lax.axis_index("z")
    core_index = lax.axis_index("core")
    tile_rows, width = matrix.shape
    part = width // layers
    halves = tile_rows // width
    vmem = pl.BlockSpec(memory_space=pltpu.VMEM)
    smem = pl.BlockSpec(memory_space=pltpu.SMEM)
    params = pltpu.CompilerParams(vmem_limit_bytes=40 * 2**20)

    left_piece = lax.dynamic_slice_in_dim(matrix, layer_index * part, part, 1).T
    right_piece = lax.dynamic_slice_in_dim(
        matrix.reshape(halves, layers, part, width), layer_index, 1, 1
    ).reshape(halves, part, width)
    right = to_all(right_piece, "row")
    left_own = jnp.concatenate(ring_of_eight(left_piece, "z"), axis=0)
    left_own, right = lax.optimization_barrier((left_own, right))
    left_other = lax.ppermute(left_own, "core", [(0, 1), (1, 0)])
    place = jnp.stack([row_index, z_index, core_index])

    depth = left_own.shape[0]
    ordered = pltpu.VMEM((rows_count, part, width), jnp.bfloat16)
    cost = pl.CostEstimate(
        flops=2 * tile_rows * width * depth, bytes_accessed=2 * depth * (tile_rows + width), transcendentals=0
    )
    own_total = pl.pallas_call(
        own_kernel,
        out_shape=jax.ShapeDtypeStruct((tile_rows, width), jnp.float32),
        in_specs=[smem] + [vmem] * 2,
        out_specs=vmem,
        scratch_shapes=[ordered],
        compiler_params=params,
        cost_estimate=cost,
    )(place, left_own, right)
    square_part = pl.pallas_call(
        square_kernel,
        out_shape=jax.ShapeDtypeStruct((layers, halves, part, width), jnp.bfloat16),
        in_specs=[smem] + [vmem] * 3,
        out_specs=pl.BlockSpec(memory_space=pltpu.HBM),
        scratch_shapes=[
            ordered,
            pltpu.VMEM((halves, layers, part, width), jnp.bfloat16),
            pltpu.SemaphoreType.DMA((halves,)),
        ],
        compiler_params=params,
        cost_estimate=cost,
    )(place, own_total, left_other, right)
    left_own, left_other, square_part = lax.optimization_barrier((left_own, left_other, square_part))
    turned = jax.ShapeDtypeStruct((tile_rows, depth), left_own.dtype)
    left_own, left_other = pl.pallas_call(
        turn_kernel,
        out_shape=[turned] * 2,
        in_specs=[vmem] * 2,
        out_specs=[vmem] * 2,
        compiler_params=params,
        cost_estimate=cost,
    )(left_own, left_other)
    parts = lax.all_to_all(square_part, "layer", split_axis=0, concat_axis=0, tiled=True)
    filtered_piece = pl.pallas_call(
        filter_kernel,
        out_shape=jax.ShapeDtypeStruct((halves, part, width), jnp.bfloat16),
        in_specs=[smem, smem, vmem],
        out_specs=vmem,
        compiler_params=params,
    )(keep_mask, layer_index.reshape(1), parts)
    filtered = ring_with_pair(filtered_piece, "row")

    scale = jnp.where(layer_index == 0, 1.5, 0.0).astype(jnp.float32).reshape(1)
    chosen = send_list[0]
    pairs = BLK * BLK // 128
    outgoing = pl.pallas_call(
        cube_kernel,
        out_shape=jax.ShapeDtypeStruct((chosen.shape[0], pairs, 128), jnp.bfloat16),
        in_specs=[smem] * 3 + [vmem] * 10,
        out_specs=vmem,
        scratch_shapes=[
            pltpu.VMEM((halves, rows_count, part, width), jnp.bfloat16),
            pltpu.VMEM((tile_rows, width), jnp.float32),
            pltpu.VMEM((4, BLK, 128), jnp.float32),
        ],
        compiler_params=params,
    )(chosen, place, scale, left_own, left_other, matrix, *filtered)
    arrived = lax.all_to_all(outgoing, ("z", "core"), split_axis=0, concat_axis=0, tiled=True)
    everyone = to_all(arrived, "layer")
    total = everyone.astype(jnp.float32).sum(0).astype(jnp.bfloat16)
    return total.reshape(total.shape[0], BLK * BLK)


def solution(mesh):
    sizes = mesh.shape
    cores = 2
    shape = (sizes["row"], sizes["col"] // cores, cores, sizes["layer"])
    split = Mesh(mesh.devices.reshape(shape), ("row", "z", "core", "layer"))
    column = ("z", "core")
    in_specs = (P("row", column), P("row", column), P(("row",) + column, None))
    out_specs = P(("row",) + column, None)
    return jax.shard_map(
        on_device, mesh=split, in_specs=in_specs, out_specs=out_specs, check_vma=False
    )
```

```python
import jax
import jax.numpy as jnp
from jax import lax
from jax.experimental import pallas as pl
from jax.experimental.pallas import tpu as pltpu
from jax.sharding import Mesh, PartitionSpec as P

BLK = 64
CONTRACT = (((0,), (0,)), ((), ()))


def to_all(piece, axis):
    copies = jnp.broadcast_to(piece[None], (lax.axis_size(axis),) + piece.shape)
    return lax.all_to_all(copies, axis, split_axis=0, concat_axis=0, tiled=True)


def shifted(piece, axis, by):
    size = lax.axis_size(axis)
    pairs = []
    for i in range(size):
        pairs.append((2 * i, 2 * ((i - by) % size)))
        pairs.append((2 * i + 1, 2 * ((i + by) % size) + 1))
    return lax.ppermute(piece, (axis, "core"), pairs)


def ring_of_eight(piece, axis):
    up = shifted(piece, axis, 2)
    down = shifted(piece, axis, -2)
    near_up = shifted(piece, axis, 1)
    near_down = shifted(piece, axis, -1)
    far_up = shifted(up, axis, 1)
    far_down = shifted(down, axis, -1)
    opposite = shifted(up, axis, 2)
    return piece, near_up, up, far_up, opposite, far_down, down, near_down


def own_kernel(place_ref, own_ref, right_ref, total_ref, ordered_ref):
    tiles, _, part, columns = right_ref.shape
    z, core = place_ref[1], place_ref[2]
    way = 1 - 2 * core
    for offset in range(tiles):
        ordered_ref[offset] = right_ref[lax.rem(z + way * offset + tiles, tiles), core]
    right = ordered_ref[...].reshape(tiles * part, columns)
    total_ref[...] = lax.dot_general(own_ref[...], right, CONTRACT, preferred_element_type=jnp.float32)


def square_kernel(place_ref, total_ref, other_ref, right_ref, out_ref, ordered_ref):
    layers, halves, part, columns = out_ref.shape
    tiles = right_ref.shape[0]
    z, core = place_ref[1], place_ref[2]
    way = 1 - 2 * core
    for offset in range(tiles):
        ordered_ref[offset] = right_ref[lax.rem(z - way * offset + tiles, tiles), 1 - core]
    right = ordered_ref[...].reshape(tiles * part, columns)
    for half in range(halves):
        rows = pl.ds(half * layers * part, layers * part)
        term = lax.dot_general(other_ref[:, rows], right, CONTRACT, preferred_element_type=jnp.float32)
        total = (total_ref[rows, :] + term).astype(out_ref.dtype)
        out_ref[:, half] = total.reshape(layers, part, columns)


def turn_kernel(own_ref, other_ref, own_turned_ref, other_turned_ref):
    own_turned_ref[...] = own_ref[...].T
    other_turned_ref[...] = other_ref[...].T


def filter_kernel(keep_ref, layer_ref, parts_ref, out_ref):
    layers, halves, part, columns = parts_ref.shape
    chunk = BLK // 2
    low = lax.broadcasted_iota(jnp.int32, (chunk, 2 * BLK), 1) < BLK
    for half in range(halves):
        for start in range(0, part, chunk):
            block = (half * layers * part + layer_ref[0] * part + start) // BLK
            rows = pl.ds(start, chunk)
            for lane in range(0, columns, 2 * BLK):
                lanes = pl.ds(lane, 2 * BLK)
                total = parts_ref[0, half, rows, lanes].astype(jnp.float32)
                for layer in range(1, layers):
                    total = total + parts_ref[layer, half, rows, lanes].astype(jnp.float32)
                left = keep_ref[block, lane // BLK].astype(jnp.float32)
                right = keep_ref[block, lane // BLK + 1].astype(jnp.float32)
                out_ref[half, rows, lanes] = (total * jnp.where(low, left, right)).astype(out_ref.dtype)


def cube_kernel(chosen_ref, place_ref, scale_ref, own_ref, other_ref, matrix_ref, *refs):
    pieces = refs[:8]
    out_ref, ordered_ref, total_ref, block_ref = refs[8:]
    owners, pairs, lanes = out_ref.shape
    half_blocks = matrix_ref.shape[1] // BLK
    tiles = ordered_ref.shape[1]
    row, z, core = place_ref[0], place_ref[1], place_ref[2]
    way = 1 - 2 * core
    for offset, piece in enumerate(pieces):
        distance = row + way * offset - z
        own = lax.rem(way * distance + 2 * tiles, tiles)
        ordered_ref[0, own] = piece[core]
        ordered_ref[1, lax.rem(tiles - own, tiles)] = piece[1 - core]
    depth, columns = own_ref.shape[1], matrix_ref.shape[1]
    total_ref[...] = jnp.dot(
        own_ref[...], ordered_ref[0].reshape(depth, columns), preferred_element_type=jnp.float32
    ) + jnp.dot(
        other_ref[...], ordered_ref[1].reshape(depth, columns), preferred_element_type=jnp.float32
    )
    low = lax.broadcasted_iota(jnp.int32, (pairs, lanes), 1) < BLK

    for owner in range(owners):
        index = chosen_ref[owner]
        live = jnp.where(index >= 0, 1.0, 0.0)
        index = jnp.maximum(index, 0)
        column = index % half_blocks
        start = pl.multiple_of(index // half_blocks * BLK, BLK)
        lane = pl.multiple_of(column // 2 * lanes, lanes)
        block = matrix_ref[pl.ds(start, BLK), pl.ds(lane, lanes)].astype(jnp.float32) * scale_ref[0]
        block = (block - 0.5 * total_ref[pl.ds(start, BLK), pl.ds(lane, lanes)]) * live
        turned = pltpu.roll(block, BLK, 1)
        odd = column % 2 == 1
        slot = 2 * (owner % 2)
        block_ref[slot] = jnp.where(odd, turned, block)
        block_ref[slot + 1] = jnp.where(odd, block, turned)
        even_rows = block_ref[slot, pl.ds(0, pairs, stride=2), :]
        odd_rows = block_ref[slot + 1, pl.ds(1, pairs, stride=2), :]
        out_ref[owner] = jnp.where(low, even_rows, odd_rows).astype(out_ref.dtype)


def on_device(matrix, keep_mask, send_list):
    layers = lax.axis_size("layer")
    rows_count = lax.axis_size("row")
    layer_index = lax.axis_index("layer")
    row_index = lax.axis_index("row")
    z_index = lax.axis_index("z")
    core_index = lax.axis_index("core")
    tile_rows, width = matrix.shape
    part = width // layers
    halves = tile_rows // width
    vmem = pl.BlockSpec(memory_space=pltpu.VMEM)
    smem = pl.BlockSpec(memory_space=pltpu.SMEM)
    params = pltpu.CompilerParams(vmem_limit_bytes=40 * 2**20)

    left_piece = lax.dynamic_slice_in_dim(matrix, layer_index * part, part, 1).T
    right_piece = lax.dynamic_slice_in_dim(
        matrix.reshape(halves, layers, part, width), layer_index, 1, 1
    ).reshape(halves, part, width)
    right = to_all(right_piece, "row")
    left_own = jnp.concatenate(ring_of_eight(left_piece, "z"), axis=0)
    left_own, right = lax.optimization_barrier((left_own, right))
    left_other = lax.ppermute(left_own, "core", [(0, 1), (1, 0)])
    place = jnp.stack([row_index, z_index, core_index])

    depth = left_own.shape[0]
    ordered = pltpu.VMEM((rows_count, part, width), jnp.bfloat16)
    cost = pl.CostEstimate(
        flops=2 * tile_rows * width * depth, bytes_accessed=2 * depth * (tile_rows + width), transcendentals=0
    )
    own_total = pl.pallas_call(
        own_kernel,
        out_shape=jax.ShapeDtypeStruct((tile_rows, width), jnp.float32),
        in_specs=[smem] + [vmem] * 2,
        out_specs=vmem,
        scratch_shapes=[ordered],
        compiler_params=params,
        cost_estimate=cost,
    )(place, left_own, right)
    square_part = pl.pallas_call(
        square_kernel,
        out_shape=jax.ShapeDtypeStruct((layers, halves, part, width), jnp.bfloat16),
        in_specs=[smem] + [vmem] * 3,
        out_specs=vmem,
        scratch_shapes=[ordered],
        compiler_params=params,
        cost_estimate=cost,
    )(place, own_total, left_other, right)
    left_own, left_other, square_part = lax.optimization_barrier((left_own, left_other, square_part))
    turned = jax.ShapeDtypeStruct((tile_rows, depth), left_own.dtype)
    left_own, left_other = pl.pallas_call(
        turn_kernel,
        out_shape=[turned] * 2,
        in_specs=[vmem] * 2,
        out_specs=[vmem] * 2,
        compiler_params=params,
        cost_estimate=cost,
    )(left_own, left_other)
    parts = lax.all_to_all(square_part, "layer", split_axis=0, concat_axis=0, tiled=True)
    filtered_piece = pl.pallas_call(
        filter_kernel,
        out_shape=jax.ShapeDtypeStruct((halves, part, width), jnp.bfloat16),
        in_specs=[smem, smem, vmem],
        out_specs=vmem,
        compiler_params=params,
    )(keep_mask, layer_index.reshape(1), parts)
    filtered = ring_of_eight(filtered_piece, "row")

    scale = jnp.where(layer_index == 0, 1.5, 0.0).astype(jnp.float32).reshape(1)
    chosen = send_list[0]
    pairs = BLK * BLK // 128
    outgoing = pl.pallas_call(
        cube_kernel,
        out_shape=jax.ShapeDtypeStruct((chosen.shape[0], pairs, 128), jnp.bfloat16),
        in_specs=[smem] * 3 + [vmem] * 11,
        out_specs=vmem,
        scratch_shapes=[
            pltpu.VMEM((halves, rows_count, part, width), jnp.bfloat16),
            pltpu.VMEM((tile_rows, width), jnp.float32),
            pltpu.VMEM((4, BLK, 128), jnp.float32),
        ],
        compiler_params=params,
    )(chosen, place, scale, left_own, left_other, matrix, *filtered)
    arrived = lax.all_to_all(outgoing, ("z", "core"), split_axis=0, concat_axis=0, tiled=True)
    everyone = to_all(arrived, "layer")
    total = everyone.astype(jnp.float32).sum(0).astype(jnp.bfloat16)
    return total.reshape(total.shape[0], BLK * BLK)


def solution(mesh):
    sizes = mesh.shape
    cores = 2
    shape = (sizes["row"], sizes["col"] // cores, cores, sizes["layer"])
    split = Mesh(mesh.devices.reshape(shape), ("row", "z", "core", "layer"))
    column = ("z", "core")
    in_specs = (P("row", column), P("row", column), P(("row",) + column, None))
    out_specs = P(("row",) + column, None)
    return jax.shard_map(
        on_device, mesh=split, in_specs=in_specs, out_specs=out_specs, check_vma=False
    )
```
